256 devices in a mesh: wave: 4 (over x), row: 8 (over z_lo, core), col: 8 (over z_hi, y).
Axes of the slice: x: 4, y: 4, z: 8 (z_hi: 2, z_lo: 4; z = z_hi * 4 + z_lo), core: 2. Of those that a mesh axis runs over, the one named last changes fastest.
Arguments:
- wavefield: float32 [2, 32, 512, 1024], P(None, 'wave', 'row', 'col'), may hold values from -6 to 6
- wavelength: float32 [32], P('wave'), may hold values from 0.45 to 0.65
- weight: float32 [32], P('wave'), may hold values from 0.25 to 1
- spectrum: float32 [2, 512, 1024], P(None, 'col', 'row'), may hold values from -5 to 5
- measured: float32 [512, 1024], P('row', 'col'), may hold values from -6 to 6
Outputs:
- field_grad: float32 [2, 32, 512, 1024], P(None, 'wave', 'row', 'col')
- residual: float32 [512, 1024], P('row', 'col')
The draws below stay inside these ranges and needn't reach their ends.
All inputs are finite; a program needn't handle non-finite values.
Results may differ from the reference program's by a relative error of at most 0.00018.
Values sent between devices are 32-bit elements; how exact they have to be, the bound alone decides.
No kernel may reach another device: no remote copies, remote signals or barrier semaphores. Data moves between devices by JAX's collectives and lax.ppermute only.
A program may use at most 64 MiB of HBM per device.

```python
import math
import jax
import jax.numpy as jnp
from jax import lax

WAVES = 32
HALO = 64
TR = 64
TC = 128
NR = 512
NC = 1024


def steps_of(own_key, shape, cuts, low, largest):
    factor_of, own = 1.0, jax.random.fold_in(own_key, 6)
    for dim, shards_of in cuts:
        draws = jnp.exp(jax.random.uniform(jax.random.fold_in(own, dim), (shards_of,), jnp.float32, low / len(cuts), largest / len(cuts)))
        factor_of = factor_of * jnp.repeat(draws, shape[dim] // shards_of).reshape([-1 if axis == dim else 1 for axis in range(len(shape))])
    return factor_of


def scatter_about(stream_key, extent, scale, reach, split=(), dtype=jnp.bfloat16):
    values = jax.random.normal(stream_key, extent, jnp.float32) * scale
    if len(split) > 0:
        values = steps_of(stream_key, extent, split, -0.22, 0.18) * values
    return jnp.clip(values, min=-reach, max=reach).astype(dtype)


def setup_inputs(seed: int = 0) -> dict:
    key_list = jax.random.split(jax.random.key(seed), 6)
    return {
        "wavefield": scatter_about(key_list[0], (2, WAVES, NR, NC), 1.0, 6.0, ((1, 4), (2, 8), (3, 8)), jnp.float32),
        "wavelength": jnp.clip(jnp.exp(math.log(0.65) - 0.36772477 * jax.random.uniform(key_list[1], (WAVES,), jnp.float32) ** steps_of(key_list[1], (WAVES,), ((0, 4),), -0.2, 0.2)), 0.45, 0.65),
        "weight": jnp.clip(jnp.exp(math.log(1.0) - 1.3862944 * jax.random.uniform(key_list[2], (WAVES,), jnp.float32) ** steps_of(key_list[2], (WAVES,), ((0, 4),), -0.2, 0.2)), 0.25, 1.0),
        "spectrum": scatter_about(key_list[3], (2, NR, NC), 0.7, 5.0, ((1, 8), (2, 8)), jnp.float32),
        "measured": scatter_about(key_list[4], (NR, NC), 1.0, 6.0, ((0, 8), (1, 8)), jnp.float32),
    }


HIGHEST = lax.Precision.HIGHEST

def tap_values(offset, wave_len):
    spread_d = jnp.arange(-HALO, HALO + 1).astype(jnp.float32)
    profile = jnp.exp(-2.0 * (spread_d / HALO) ** 2)
    norm_scale = 1.0 / jnp.sqrt(jnp.sum(profile))
    amplitude = jnp.exp(-(offset / HALO) ** 2) * norm_scale
    phase = offset * offset / (2.0 * wave_len * HALO)
    inside = jnp.abs(offset) <= HALO
    return (jnp.where(inside, amplitude * jnp.cos(phase), 0.0), jnp.where(inside, amplitude * jnp.sin(phase), 0.0))

def toeplitz(length, wave_len, conj_sign):
    row_index = jnp.arange(length + 2 * HALO)[:, None]
    col_index = jnp.arange(length)[None, :]
    offset = (row_index - col_index - HALO).astype(jnp.float32)
    real_part, imag_part = tap_values(offset, wave_len)
    return (real_part, conj_sign * imag_part)

def band_last(data_re, data_im, table_re, table_im, block_len):
    num_blocks = (data_re.shape[-1] - 2 * HALO) // block_len
    pieces_re = []
    pieces_im = []
    for position in range(num_blocks):
        window_re = data_re[:, position * block_len:position * block_len + block_len + 2 * HALO]
        window_im = data_im[:, position * block_len:position * block_len + block_len + 2 * HALO]
        pieces_re.append(jnp.dot(window_re, table_re, precision=HIGHEST) - jnp.dot(window_im, table_im, precision=HIGHEST))
        pieces_im.append(jnp.dot(window_re, table_im, precision=HIGHEST) + jnp.dot(window_im, table_re, precision=HIGHEST))
    return (jnp.concatenate(pieces_re, axis=1), jnp.concatenate(pieces_im, axis=1))

def propagate(field_re, field_im, wave_len, conj_sign):
    col_re, col_im = toeplitz(TC, wave_len, conj_sign)
    row_re, row_im = toeplitz(TR, wave_len, conj_sign)
    padded_re = jnp.pad(field_re, HALO)
    padded_im = jnp.pad(field_im, HALO)
    middle_re, middle_im = band_last(padded_re, padded_im, col_re, col_im, TC)
    result_re, result_im = band_last(middle_re.T, middle_im.T, row_re, row_im, TR)
    return (result_re.T, result_im.T)

def reference(wavefield, wavelength, weight, spectrum, measured):

    def illuminate(summed, entries):
        field_re, field_im, wave_len, strength = entries
        prop_re, prop_im = propagate(field_re, field_im, wave_len, 1.0)
        return (summed + strength * (prop_re * prop_re + prop_im * prop_im), None)
    zeros_grid = jnp.zeros((NR, NC), jnp.float32)
    summed, unused = lax.scan(illuminate, zeros_grid, (wavefield[0], wavefield[1], wavelength, weight))
    intensity = summed / WAVES
    transfer = spectrum[0] + 1j * spectrum[1]
    blurred = jnp.real(jnp.fft.ifft2(jnp.fft.fft2(intensity) * transfer))
    residual = (blurred - measured).astype(jnp.float32)
    pulled = jnp.real(jnp.fft.ifft2(jnp.fft.fft2(residual) * jnp.conj(transfer))).astype(jnp.float32)

    def backward(entries):
        field_re, field_im, wave_len, strength = entries
        prop_re, prop_im = propagate(field_re, field_im, wave_len, 1.0)
        grad_re, grad_im = propagate(2.0 * strength * pulled * prop_re, 2.0 * strength * pulled * prop_im, wave_len, -1.0)
        return jnp.stack([grad_re, grad_im])
    gradients = lax.map(backward, (wavefield[0], wavefield[1], wavelength, weight))
    return (jnp.transpose(gradients, (1, 0, 2, 3)), residual)
```

```python
import functools

import jax
import jax.numpy as jnp
import ml_dtypes
import numpy as np
from jax import lax
from jax.experimental import pallas as pl
from jax.experimental.pallas import tpu as pltpu
from jax.sharding import PartitionSpec as P

WAVES = 32
HALO = 64
TR = 64
TC = 128
NR = 512
NC = 1024
NW = 4
NROW = 8
NCOL = 8
LW = WAVES // NW
QC = TC // NW
KB = NR // (NCOL * NW)
F32 = jnp.float32
BF16 = jnp.bfloat16
VMEM_LIMIT = 48 * 1024 * 1024


def halves_of(table):
    high = table.astype(ml_dtypes.bfloat16)
    low = (table - high.astype(np.float64)).astype(ml_dtypes.bfloat16)
    return high, low


@functools.lru_cache(None)
def row_dft_table():
    group, block, inner = np.meshgrid(np.arange(4), np.arange(NROW), np.arange(16), indexing="ij")
    rows = (TR * block + 16 * group + inner).reshape(-1)
    angle = 2 * np.pi * (np.arange(NR)[:, None] * rows[None, :] % NR) / NR
    return halves_of(np.concatenate([np.cos(angle), -np.sin(angle)], axis=1))


@functools.lru_cache(None)
def col_dft_table():
    freq = np.arange(NC).reshape(NROW, 1, TC)
    angle = 2 * np.pi * (np.arange(NC)[None, :, None] * freq % NC) / NC
    return halves_of(np.concatenate([np.cos(angle), np.sin(angle)], axis=2))


@functools.lru_cache(None)
def col_inverse_table():
    angle = 2 * np.pi * (np.arange(NC)[:, None] * np.arange(NC)[None, :] % NC) / NC
    angle = angle.reshape(NC, 16, 1, 64)
    table = np.concatenate([np.cos(angle), np.sin(angle)], axis=2)
    return halves_of(table.reshape(NC, 2 * NC))


@functools.lru_cache(None)
def row_inverse_table():
    rows = (TR * np.arange(NROW)[:, None] - HALO + np.arange(TR + 2 * HALO)[None, :]) % NR
    angle = 2 * np.pi * (rows[:, :, None] * np.arange(NR)[None, None, :] % NR) / NR
    return halves_of(np.concatenate([np.cos(angle), np.sin(angle)], axis=1))


def split(values):
    high = values.astype(BF16)
    return high, (values - high.astype(F32)).astype(BF16)


def mm(left, right):
    return jnp.dot(left, right, preferred_element_type=F32)


def mm3(left, right):
    return mm(left[0], right[0]) + (mm(left[1], right[0]) + mm(left[0], right[1]))


def lane_ids(rows, lanes=128):
    return lax.broadcasted_iota(jnp.int32, (rows, lanes), 1)


def swapped(values):
    return pltpu.roll(values, 64, 1)


def column_taps(base):
    wide = jnp.broadcast_to(base, (128, 256))
    own = pltpu.roll(wide, 0, 1, stride=1, stride_axis=0)[:, :128]
    left = pltpu.roll(wide[:64], 256 - 64, 1, stride=1, stride_axis=0)[:, :128]
    right = pltpu.roll(wide[:64], 128, 1, stride=1, stride_axis=0)[:, :128]
    return jnp.concatenate([own, left, right], axis=0)


def row_taps(base):
    wide = jnp.broadcast_to(base, (64, 256))
    return pltpu.roll(wide, 64, 1, stride=1, stride_axis=0)[:, :192]


def column_pass(parts_re, parts_im, base_re, base_im):
    rows = parts_re[0].shape[0]
    field = jnp.concatenate(
        [jnp.concatenate(parts_re, axis=1), jnp.concatenate(parts_im, axis=1)], axis=0
    )
    table = jnp.concatenate([column_taps(base_re), column_taps(base_im)], axis=1)
    mix = mm3(split(field), split(table))
    return (
        mix[:rows, :128] - mix[rows:, 128:],
        mix[:rows, 128:] + mix[rows:, :128],
    )


def row_pass(stacked, base_re, base_im):
    table = jnp.concatenate([row_taps(base_re), row_taps(base_im)], axis=0)
    mix = mm3(split(table), split(stacked))
    return mix[:64, :128] - mix[64:, 128:], mix[:64, 128:] + mix[64:, :128]


def edges(re_part, im_part):
    lane = lane_ids(64)
    return (
        jnp.where(lane < 64, re_part, swapped(im_part)),
        jnp.where(lane < 64, swapped(re_part), im_part),
    )


def halo_parts(from_left, from_right):
    lane = lane_ids(from_left.shape[0])
    return (
        jnp.where(lane < 64, from_left, swapped(from_right)),
        jnp.where(lane < 64, swapped(from_left), from_right),
    )


def quarter(block, which):
    lane = lane_ids(16)
    out = jnp.zeros((16, 128), F32)
    for group in range(4):
        amount = lax.rem(32 * group - 32 * which + 128, 128)
        moved = pltpu.roll(block[16 * group : 16 * group + 16], amount, 1)
        out = jnp.where(lane // 32 == group, moved, out)
    return out


def pack_kernel(place_ref, field_ref, measured_ref, left_ref, right_ref, share_ref):
    for wave in range(LW):
        left, right = edges(field_ref[0, wave], field_ref[1, wave])
        left_ref[wave] = left
        right_ref[wave] = right
    share_ref[...] = jnp.broadcast_to(
        quarter(measured_ref[...], place_ref[0])[None], share_ref.shape
    )


def columns_kernel(field_ref, left_ref, right_ref, base_re_ref, base_im_ref, out_ref):
    halo_re, halo_im = halo_parts(left_ref[0], right_ref[0])
    re_out, im_out = column_pass(
        (field_ref[0, 0], halo_re), (field_ref[1, 0], halo_im), base_re_ref[0], base_im_ref[0]
    )
    out_ref[0, 0] = re_out
    out_ref[1, 0] = im_out


def rows_kernel(
    weight_ref, up_ref, own_ref, down_ref, base_re_ref, base_im_ref,
    out_ref, left_ref, right_ref, share_ref, total_ref,
):
    wave = pl.program_id(0)
    stacked = jnp.concatenate(
        [
            jnp.concatenate([ref[0, 0], ref[1, 0]], axis=1)
            for ref in (up_ref, own_ref, down_ref)
        ],
        axis=0,
    )
    re_out, im_out = row_pass(stacked, base_re_ref[0], base_im_ref[0])
    out_ref[0, 0] = re_out
    out_ref[1, 0] = im_out
    left, right = edges(re_out, im_out)
    left_ref[0] = left
    right_ref[0] = right
    term = weight_ref[wave] * (re_out * re_out + im_out * im_out)

    @pl.when(wave == 0)
    def _():
        total_ref[...] = term

    @pl.when(wave > 0)
    def _():
        total_ref[...] += term

    @pl.when(wave == LW - 1)
    def _():
        block = total_ref[...] * (1.0 / WAVES)
        for target in range(NW):
            piece = quarter(block, target)
            share_ref[pl.ds(target * NROW, NROW)] = jnp.broadcast_to(
                piece[None], (NROW, 16, 128)
            )


def row_dft_kernel(image_ref, measured_ref, high_ref, low_ref, out_ref):
    summed = image_ref[0:NROW] + image_ref[NROW : 2 * NROW]
    summed = summed + image_ref[2 * NROW : 3 * NROW]
    summed = (summed + image_ref[3 * NROW : 4 * NROW]).reshape(128, 128)
    known = measured_ref[...].reshape(128, 128)
    lane = lane_ids(128) // 32
    top = []
    low = []
    for group in range(4):
        first = pltpu.roll(summed, (128 - 32 * group) % 128, 1)
        third = pltpu.roll(known, (192 - 32 * group) % 128, 1)
        both = jnp.where(lane == 0, first, jnp.where(lane == 2, third, 0.0))
        top.append(both)
        low.append(pltpu.roll(both, 32, 1))
    operand = split(jnp.concatenate(top + low, axis=0))
    out_ref[...] = mm3((high_ref[...], low_ref[...]), operand).reshape(out_ref.shape)


def filter_kernel(place_ref, rows_ref, high_ref, low_ref, spec_re_ref, spec_im_ref, out_ref):
    lane = lane_ids(16) // 32
    channels = []
    for channel in range(4):
        pieces = []
        for col in range(NCOL):
            piece = jnp.zeros((16, 128), F32)
            for wave in range(NW):
                moved = pltpu.roll(rows_ref[col * NW + wave], (32 * (wave - channel)) % 128, 1)
                piece = jnp.where(lane == wave, moved, piece)
            pieces.append(piece)
        channels.append(jnp.concatenate(pieces, axis=1))
    operand = split(jnp.concatenate(channels, axis=0))
    mix = mm3(operand, (high_ref[0], low_ref[0]))
    image_re = mix[0:16, :128] + mix[16:32, 128:]
    image_im = mix[16:32, :128] - mix[0:16, 128:]
    known_re = mix[32:48, :128] + mix[48:64, 128:]
    known_im = mix[48:64, :128] - mix[32:48, 128:]
    spec_re, spec_im = spec_re_ref[...], spec_im_ref[...]
    blur_re = image_re * spec_re - image_im * spec_im
    blur_im = image_re * spec_im + image_im * spec_re
    rest_re = blur_re - known_re
    rest_im = blur_im - known_im
    pull_re = rest_re * spec_re + rest_im * spec_im
    pull_im = rest_im * spec_re - rest_re * spec_im
    scale = 1.0 / (NR * NC)
    both = jnp.concatenate([blur_re - pull_im, blur_im + pull_re], axis=0) * scale
    out_ref[...] = jnp.broadcast_to(both[None], out_ref.shape)


def col_inverse_kernel(rows_ref, high_ref, low_ref, out_ref):
    step = pl.program_id(0)
    operand = split(jnp.concatenate([rows_ref[block] for block in range(NROW)], axis=1))
    mix = mm3(operand, (high_ref[...], low_ref[...]))
    lane = lane_ids(16)
    for half in range(2):
        part = mix[:, 128 * half : 128 * half + 128]
        other = swapped(part[16:])
        piece = part[:16] + jnp.where(lane < 64, -other, other)
        if half == 0:
            targets = (step * NW + 1, lax.rem(step + 7, 8) * NW + 3)
        else:
            targets = (lax.rem(step + 1, 8) * NW, step * NW + 2)
        for target in targets:
            out_ref[target] = piece


def row_inverse_kernel(place_ref, rows_ref, high_ref, low_ref, out_ref):
    operand = split(rows_ref[...].reshape(NR, 128))
    mix = mm3((high_ref[0], low_ref[0]), operand)
    cos_part, sin_part = mix[:192], mix[192:]
    pulled = sin_part + swapped(cos_part)
    blurred = cos_part[64:128] - swapped(sin_part[64:128])
    low = lane_ids(96) < 64
    packed = jnp.where(low, pulled[:96], swapped(pulled[96:]))
    packed_blur = jnp.where(low[:32], blurred[:32], swapped(blurred[32:]))
    both = jnp.concatenate([packed, packed_blur], axis=0)
    out_ref[...] = jnp.broadcast_to(both[None], out_ref.shape)


def gradient_kernel(
    weight_ref, own_ref, left_ref, right_ref, up_ref, up_halo_ref, down_ref, down_halo_ref,
    images_ref, measured_ref, base_re_ref, base_im_ref, out_ref, residual_ref,
):
    wave = pl.program_id(0)
    low = lane_ids(96) < 64

    def joined(first, second):
        one, two = images_ref[first], images_ref[second]
        return (
            jnp.concatenate(
                [
                    jnp.where(low, one[:96], swapped(two[:96])),
                    jnp.where(low, swapped(one[:96]), two[:96]),
                ],
                axis=0,
            ),
            jnp.concatenate(
                [
                    jnp.where(low[:32], one[96:], swapped(two[96:])),
                    jnp.where(low[:32], swapped(one[96:]), two[96:]),
                ],
                axis=0,
            ),
        )

    centre, blurred = joined(1, 2)
    border, unused = joined(0, 3)

    @pl.when(wave == 0)
    def _():
        residual_ref[...] = blurred - measured_ref[...]

    factor = 2.0 * weight_ref[wave]
    centre = centre * factor
    border = border * factor
    halos = [
        halo_parts(up_halo_ref[0, 0], up_halo_ref[1, 0]),
        halo_parts(left_ref[0], right_ref[0]),
        halo_parts(down_halo_ref[0, 0], down_halo_ref[1, 0]),
    ]
    parts = []
    for part, sign in ((0, 1.0), (1, -1.0)):
        own = jnp.concatenate([up_ref[part, 0], own_ref[part, 0], down_ref[part, 0]], axis=0)
        halo = jnp.concatenate([pair[part] for pair in halos], axis=0)
        parts.append((sign * (own * centre), sign * (halo * border)))
    re_mid, im_mid = column_pass(parts[0], parts[1], base_re_ref[0], base_im_ref[0])
    re_out, im_out = row_pass(
        jnp.concatenate([re_mid, im_mid], axis=1), base_re_ref[0], base_im_ref[0]
    )
    out_ref[0, 0] = re_out
    out_ref[1, 0] = -im_out


def params():
    return pltpu.CompilerParams(vmem_limit_bytes=VMEM_LIMIT)


def shape(*dims):
    return jax.ShapeDtypeStruct(dims, F32)


SMEM = pl.BlockSpec(memory_space=pltpu.SMEM)


def per_wave(*block):
    if len(block) == 4:
        return pl.BlockSpec(block, lambda w: (0, w, 0, 0))
    return pl.BlockSpec(block, lambda w: (w, 0, 0))


def whole(*block):
    return pl.BlockSpec(block, lambda *unused: (0,) * len(block))


def neighbours(value, axis, count, step):
    return lax.ppermute(
        value, axis, [(i, i + step) for i in range(count) if 0 <= i + step < count]
    )


def mirrored_spectrum(spectrum):
    def mirror(value, axis, dim):
        size = value.shape[dim]
        rest = lax.ppermute(value, axis, [(i, 7 - i) for i in range(8)])
        edge = lax.ppermute(
            lax.slice_in_dim(value, 0, 1, axis=dim), axis, [(i, (8 - i) % 8) for i in range(8)]
        )
        rest = lax.rev(lax.slice_in_dim(rest, 1, size, axis=dim), (dim,))
        return jnp.concatenate([edge, rest], axis=dim)

    return mirror(mirror(spectrum, "col", 1), "row", 2)


def taps_of(wavelength):
    lane = jnp.arange(256)
    offset = jnp.where(lane < 128, lane, lane - 256).astype(F32)
    spread = jnp.arange(-HALO, HALO + 1).astype(F32)
    norm = 1.0 / jnp.sqrt(jnp.sum(jnp.exp(-2.0 * (spread / HALO) ** 2)))
    amplitude = jnp.where(jnp.abs(offset) <= HALO, jnp.exp(-((offset / HALO) ** 2)) * norm, 0.0)
    phase = offset * offset / (2.0 * wavelength[:, None] * HALO)
    return (amplitude * jnp.cos(phase))[:, None, :], (amplitude * jnp.sin(phase))[:, None, :]


def shards(wavefield, wavelength, weight, spectrum, measured):
    wave_place = lax.axis_index("wave")
    row_place = lax.axis_index("row")[None]

    left_edge, right_edge, known_share = pl.pallas_call(
        pack_kernel,
        in_specs=[SMEM, pl.BlockSpec(), pl.BlockSpec()],
        out_shape=(shape(LW, 64, 128), shape(LW, 64, 128), shape(NROW, 16, 128)),
        compiler_params=params(),
    )(wave_place[None], wavefield, measured)
    from_left = neighbours(right_edge, "col", NCOL, 1)
    from_right = neighbours(left_edge, "col", NCOL, -1)

    base_re, base_im = taps_of(wavelength)
    base_specs = [per_wave(1, 1, 256), per_wave(1, 1, 256)]
    mirror = mirrored_spectrum(spectrum)
    spec_re = 0.5 * (spectrum[0] + mirror[0])
    spec_im = 0.5 * (spectrum[1] - mirror[1])
    spec_re = lax.dynamic_slice_in_dim(spec_re, wave_place * KB, KB, 0)
    spec_im = lax.dynamic_slice_in_dim(spec_im, wave_place * KB, KB, 0)
    known = lax.all_to_all(known_share, "row", split_axis=0, concat_axis=0, tiled=True)

    middle = pl.pallas_call(
        columns_kernel,
        grid=(LW,),
        in_specs=[per_wave(2, 1, 64, 128), per_wave(1, 64, 128), per_wave(1, 64, 128)] + base_specs,
        out_specs=per_wave(2, 1, 64, 128),
        out_shape=shape(2, LW, 64, 128),
        compiler_params=params(),
    )(wavefield, from_left, from_right, base_re, base_im)
    from_up = neighbours(middle, "row", NROW, 1)
    from_down = neighbours(middle, "row", NROW, -1)
    propagated, left_edge, right_edge, shares = pl.pallas_call(
        rows_kernel,
        grid=(LW,),
        in_specs=[SMEM] + [per_wave(2, 1, 64, 128)] * 3 + base_specs,
        out_specs=(
            per_wave(2, 1, 64, 128),
            per_wave(1, 64, 128),
            per_wave(1, 64, 128),
            whole(NW * NROW, 16, 128),
        ),
        out_shape=(
            shape(2, LW, 64, 128),
            shape(LW, 64, 128),
            shape(LW, 64, 128),
            shape(NW * NROW, 16, 128),
        ),
        scratch_shapes=[pltpu.VMEM((64, 128), F32)],
        compiler_params=params(),
    )(weight, from_up, middle, from_down, base_re, base_im)

    prop_left = neighbours(right_edge, "col", NCOL, 1)
    prop_right = neighbours(left_edge, "col", NCOL, -1)
    prop_up = neighbours(propagated, "row", NROW, 1)
    prop_down = neighbours(propagated, "row", NROW, -1)
    sides = jnp.stack([prop_left, prop_right])
    up_sides = neighbours(sides, "row", NROW, 1)
    down_sides = neighbours(sides, "row", NROW, -1)

    image = lax.all_to_all(shares, ("wave", "row"), split_axis=0, concat_axis=0, tiled=True)
    high, low = row_dft_table()
    freq_rows = pl.pallas_call(
        row_dft_kernel,
        out_shape=shape(NCOL * NW, 16, 128),
        compiler_params=params(),
    )(image, known, jnp.asarray(high), jnp.asarray(low))
    freq_rows = lax.all_to_all(freq_rows, ("col", "wave"), split_axis=0, concat_axis=0, tiled=True)

    high, low = col_dft_table()
    table_spec = pl.BlockSpec((1, NC, 256), lambda i, place: (place[0], 0, 0))
    filtered = pl.pallas_call(
        filter_kernel,
        grid_spec=pltpu.PrefetchScalarGridSpec(
            num_scalar_prefetch=1,
            grid=(1,),
            in_specs=[
                whole(NCOL * NW, 16, 128), table_spec, table_spec, whole(KB, 128), whole(KB, 128),
            ],
            out_specs=whole(NROW, 2 * KB, 128),
        ),
        out_shape=shape(NROW, 2 * KB, 128),
        compiler_params=params(),
    )(row_place, freq_rows, jnp.asarray(high), jnp.asarray(low), spec_re, spec_im)
    filtered = lax.all_to_all(filtered, "row", split_axis=0, concat_axis=0, tiled=True)

    high, low = col_inverse_table()
    table_spec = pl.BlockSpec((NC, 256), lambda i: (0, i))
    columns = pl.pallas_call(
        col_inverse_kernel,
        grid=(8,),
        in_specs=[whole(NROW, 2 * KB, 128), table_spec, table_spec],
        out_specs=whole(NCOL * NW, 16, 128),
        out_shape=shape(NCOL * NW, 16, 128),
        compiler_params=params(),
    )(filtered, jnp.asarray(high), jnp.asarray(low))
    columns = lax.all_to_all(columns, ("col", "wave"), split_axis=0, concat_axis=0, tiled=True)

    high, low = row_inverse_table()
    table_spec = pl.BlockSpec((1, 384, NR), lambda i, place: (place[0], 0, 0))
    images = pl.pallas_call(
        row_inverse_kernel,
        grid_spec=pltpu.PrefetchScalarGridSpec(
            num_scalar_prefetch=1,
            grid=(1,),
            in_specs=[whole(NCOL * NW, 16, 128), table_spec, table_spec],
            out_specs=whole(NW, 128, 128),
        ),
        out_shape=shape(NW, 128, 128),
        compiler_params=params(),
    )(row_place, columns, jnp.asarray(high), jnp.asarray(low))
    images = lax.all_to_all(images, "wave", split_axis=0, concat_axis=0, tiled=True)

    field_grad, residual = pl.pallas_call(
        gradient_kernel,
        grid=(LW,),
        in_specs=[
            SMEM,
            per_wave(2, 1, 64, 128),
            per_wave(1, 64, 128),
            per_wave(1, 64, 128),
            per_wave(2, 1, 64, 128),
            per_wave(2, 1, 64, 128),
            per_wave(2, 1, 64, 128),
            per_wave(2, 1, 64, 128),
            whole(NW, 128, 128),
            whole(64, 128),
        ] + base_specs,
        out_specs=(per_wave(2, 1, 64, 128), whole(64, 128)),
        out_shape=(shape(2, LW, 64, 128), shape(64, 128)),
        compiler_params=params(),
    )(
        weight, propagated, prop_left, prop_right, prop_up, up_sides, prop_down, down_sides,
        images, measured, base_re, base_im,
    )
    return field_grad, residual


def solution(mesh):
    placed = (
        P(None, "wave", "row", "col"),
        P("wave"),
        P("wave"),
        P(None, "col", "row"),
        P("row", "col"),
    )
    return jax.shard_map(
        shards,
        mesh=mesh,
        in_specs=placed,
        out_specs=(P(None, "wave", "row", "col"), P("row", "col")),
        check_vma=False,
    )
```

```python
import functools

import jax
import jax.numpy as jnp
import ml_dtypes
import numpy as np
from jax import lax
from jax.experimental import pallas as pl
from jax.experimental.pallas import tpu as pltpu
from jax.sharding import PartitionSpec as P

WAVES = 32
HALO = 64
TR = 64
TC = 128
NR = 512
NC = 1024
NW = 4
NROW = 8
NCOL = 8
LW = WAVES // NW
QC = TC // NW
KB = NR // (NCOL * NW)
STEP = 2
HALO_BYTES = 1 << 27
ROOT = float(np.sqrt(0.5))
F32 = jnp.float32
BF16 = jnp.bfloat16
VMEM_LIMIT = 20 * 1024 * 1024


def halves_of(table):
    high = table.astype(ml_dtypes.bfloat16)
    low = (table - high.astype(np.float64)).astype(ml_dtypes.bfloat16)
    return high, low


@functools.lru_cache(None)
def row_dft_table():
    group, block, inner = np.meshgrid(np.arange(4), np.arange(NROW), np.arange(16), indexing="ij")
    rows = (TR * block + 16 * group + inner).reshape(-1)
    angle = 2 * np.pi * (np.arange(NR)[:, None] * rows[None, :] % NR) / NR
    return halves_of(np.concatenate([np.cos(angle), -np.sin(angle)], axis=1))


@functools.lru_cache(None)
def col_dft_table():
    freq = (8 * np.arange(128)[None, :] + np.arange(8)[:, None])[:, None, :]
    angle = 2 * np.pi * (np.arange(128)[None, :, None] * freq % NC) / NC
    return halves_of(np.concatenate([np.cos(angle), np.sin(angle)], axis=2))


@functools.lru_cache(None)
def col_inverse_table():
    freq = (8 * np.arange(128)[None, :] + np.arange(8)[:, None])[:, :, None]
    angle = 2 * np.pi * (np.arange(128)[None, None, :] * freq % NC) / NC
    return halves_of(np.concatenate([np.cos(angle), np.sin(angle)], axis=2))


@functools.lru_cache(None)
def column_order():
    table = np.zeros((128, 128))
    for m in range(16):
        for n in range(8):
            table[8 * m + n, 16 * n + m] = 1.0
    return table.astype(ml_dtypes.bfloat16)


@functools.lru_cache(None)
def row_inverse_table():
    rows = TR * np.arange(NROW)[:, None] + np.arange(TR)[None, :]
    angle = 2 * np.pi * (rows[:, :, None] * np.arange(NR)[None, None, :] % NR) / NR
    return halves_of(np.concatenate([np.cos(angle), np.sin(angle)], axis=1))


def split(values):
    high = values.astype(BF16)
    return high, (values - high.astype(F32)).astype(BF16)


def mm(left, right):
    return jnp.dot(left, right, preferred_element_type=F32)


def mm3(left, right):
    rows = left[0].shape[0]
    most = mm(jnp.concatenate(left, axis=0), right[0])
    return most[:rows] + (most[rows:] + mm(left[0], right[1]))


def three(values):
    high = values.astype(BF16)
    middle, low = split(values - high.astype(F32))
    return high, middle, low


def lane_ids(rows, lanes=128):
    return lax.broadcasted_iota(jnp.int32, (rows, lanes), 1)


def swapped(values):
    return pltpu.roll(values, 64, 1)


def column_taps(base):
    wide = jnp.broadcast_to(base, (128, 256))
    own = pltpu.roll(wide, 0, 1, stride=1, stride_axis=0)[:, :128]
    left = pltpu.roll(wide[:64], 256 - 64, 1, stride=1, stride_axis=0)[:, :128]
    right = pltpu.roll(wide[:64], 128, 1, stride=1, stride_axis=0)[:, :128]
    return jnp.concatenate([own, left, right], axis=0)


def row_taps(base):
    wide = jnp.broadcast_to(base, (64, 256))
    return pltpu.roll(wide, 64, 1, stride=1, stride_axis=0)[:, :192]


def column_pass(parts_re, parts_im, table):
    rows = parts_re[0].shape[0]
    field = jnp.concatenate(
        [jnp.concatenate(parts_re, axis=1), jnp.concatenate(parts_im, axis=1)], axis=0
    )
    mix = mm3(split(field), table)
    return (
        mix[:rows, :128] - mix[rows:, 128:],
        mix[:rows, 128:] + mix[rows:, :128],
    )


def row_pass(stacked, table):
    mix = mm3(table, split(stacked))
    return mix[:64, :128] - mix[64:, 128:], mix[:64, 128:] + mix[64:, :128]


def over_waves(step):
    def body(start, carry):
        for wave in range(STEP):
            step(start * STEP + wave)
        return carry

    lax.fori_loop(0, LW // STEP, body, 0)


def edges(re_part, im_part):
    lane = lane_ids(re_part.shape[0])
    return (
        jnp.where(lane < 64, re_part, swapped(im_part)),
        jnp.where(lane < 64, swapped(re_part), im_part),
    )


def halo_parts(from_left, from_right):
    lane = lane_ids(from_left.shape[0])
    return (
        jnp.where(lane < 64, from_left, swapped(from_right)),
        jnp.where(lane < 64, swapped(from_left), from_right),
    )


def quarter(block, which):
    lane = lane_ids(16)
    out = jnp.zeros((16, 128), F32)
    for group in range(4):
        amount = lax.rem(32 * group - 32 * which + 128, 128)
        moved = pltpu.roll(block[16 * group : 16 * group + 16], amount, 1)
        out = jnp.where(lane // 32 == group, moved, out)
    return out


def fetch(pairs, sems):
    copies = [
        pltpu.make_async_copy(source, target, sems.at[i])
        for i, (source, target) in enumerate(pairs)
    ]
    for copy in copies:
        copy.start()
    return copies


def load_kernel(place_ref, table_ref, out_ref, sems):
    for copy in fetch([(table_ref.at[place_ref[0]], out_ref)], sems):
        copy.wait()


def pack_kernel(field_ref, held_ref, left_ref, right_ref, sems):
    copies = fetch([(field_ref.at[:, wave], held_ref.at[:, wave]) for wave in range(LW)], sems)
    for wave in range(LW):
        copies[wave].wait()
        left, right = edges(held_ref[0, wave], held_ref[1, wave])
        left_ref[wave] = left
        right_ref[wave] = right


def mirror_kernel(
    place_ref, measured_ref, spec_ref, after_ref, share_ref, mirror_ref, first_ref,
    measured_in, spec_in, sems,
):
    copies = fetch([(spec_ref, spec_in), (measured_ref, measured_in)], sems)
    place = place_ref[0]
    row = lax.broadcasted_iota(jnp.int32, (16, 64), 0)
    pick = (lane_ids(16, 64) == 64 - KB * place - row).astype(BF16)
    copies[0].wait()
    start = pl.multiple_of(place * KB, KB)
    for part in range(2):
        mirror_ref[part] = sum(mm(pick, piece) for piece in three(spec_in[part]))
        first_ref[part] = spec_in[part, 0:8]
        share_ref[16 + 16 * part : 32 + 16 * part] = spec_in[part, pl.ds(start, KB)]
    copies[1].wait()
    share_ref[0:16] = quarter(measured_in[...], place)


def share_kernel(place_ref, share_ref, mirror_ref, first_ref, out_ref):
    place = place_ref[0]
    top = lax.broadcasted_iota(jnp.int32, (16, 128), 0) == 0
    rows = [share_ref[...]]
    for part in range(2):
        other = jnp.broadcast_to(first_ref[part, 0:1], (16, 128))
        rows.append(jnp.where(jnp.logical_and(top, place == 0), other, mirror_ref[part]))
    out_ref[...] = jnp.broadcast_to(jnp.concatenate(rows, axis=0)[None], out_ref.shape)


def order_kernel(rows_ref, order_ref, reverse_ref, out_ref):
    order, reverse = order_ref[...], reverse_ref[...]
    lane = lane_ids(64) // 16
    parts = []
    for row in range(NROW):
        parts.append(sum(mm(piece, order) for piece in three(rows_ref[row, 16:80])))
    ordered = []
    for n in range(8):
        out = jnp.zeros((64, 128), F32)
        for row in range(NROW):
            moved = pltpu.roll(parts[row], (16 * (row - n)) % 128, 1)
            out = jnp.where(lane == row, moved, out)
        ordered.append(out)
    for n in range(8):
        back = sum(mm(piece, reverse) for piece in three(ordered[(8 - n) % 8][32:]))
        if n == 0:
            back = pltpu.roll(back, 1, 1)
        out_ref[n, 0:16] = 0.5 * (ordered[n][0:16] + back[0:16])
        out_ref[n, 16:32] = 0.5 * (ordered[n][16:32] - back[16:32])


def column_tables(base_re_ref, base_im_ref, high_ref, low_ref):
    for wave in range(LW):
        high_ref[wave], low_ref[wave] = split(
            jnp.concatenate(
                [column_taps(base_re_ref[wave]), column_taps(base_im_ref[wave])], axis=1
            )
        )


def row_tables(base_re_ref, base_im_ref, high_ref, low_ref):
    for wave in range(LW):
        high_ref[wave], low_ref[wave] = split(
            jnp.concatenate([row_taps(base_re_ref[wave]), row_taps(base_im_ref[wave])], axis=0)
        )


def columns_kernel(
    field_ref, left_ref, right_ref, base_re_ref, base_im_ref, after_ref, out_ref, high_ref, low_ref
):
    column_tables(base_re_ref, base_im_ref, high_ref, low_ref)

    def step(wave):
        halo_re, halo_im = halo_parts(left_ref[wave], right_ref[wave])
        out_ref[0, wave], out_ref[1, wave] = column_pass(
            (field_ref[0, wave], halo_re),
            (field_ref[1, wave], halo_im),
            (high_ref[wave], low_ref[wave]),
        )

    over_waves(step)


def stacked_rows(refs, wave):
    return jnp.concatenate(
        [jnp.concatenate([ref[0, wave], ref[1, wave]], axis=1) for ref in refs], axis=0
    )


def rows_kernel(
    weight_ref, up_ref, own_ref, down_ref, base_re_ref, base_im_ref,
    out_ref, left_ref, right_ref, share_ref, total_ref, high_ref, low_ref,
):
    row_tables(base_re_ref, base_im_ref, high_ref, low_ref)
    total_ref[...] = jnp.zeros_like(total_ref)

    def step(wave):
        re_out, im_out = row_pass(
            stacked_rows((up_ref, own_ref, down_ref), wave), (high_ref[wave], low_ref[wave])
        )
        out_ref[0, wave] = re_out
        out_ref[1, wave] = im_out
        left, right = edges(re_out, im_out)
        left_ref[wave] = left
        right_ref[wave] = right
        total_ref[...] += weight_ref[wave] * (re_out * re_out + im_out * im_out)

    over_waves(step)
    block = total_ref[...] * (1.0 / WAVES)
    for target in range(NW):
        piece = quarter(block, target)
        share_ref[target * NROW : (target + 1) * NROW] = jnp.broadcast_to(
            piece[None], (NROW, 16, 128)
        )


def row_dft_kernel(image_ref, measured_ref, table_ref, out_ref):
    summed = image_ref[0:NROW] + image_ref[NROW : 2 * NROW]
    summed = summed + image_ref[2 * NROW : 3 * NROW]
    summed = (summed + image_ref[3 * NROW : 4 * NROW]).reshape(128, 128)
    known = measured_ref[:, 0:16].reshape(128, 128)
    lane = lane_ids(128) // 32
    top = []
    low = []
    for group in range(4):
        first = pltpu.roll(summed, (128 - 32 * group) % 128, 1)
        third = pltpu.roll(known, (192 - 32 * group) % 128, 1)
        both = jnp.where(lane == 0, first, jnp.where(lane == 2, third, 0.0))
        top.append(both)
        low.append(pltpu.roll(both, 32, 1))
    operand = split(jnp.concatenate(top + low, axis=0))
    out_ref[...] = mm3((table_ref[0], table_ref[1]), operand).reshape(out_ref.shape)


def eight_point(terms, sign):
    if len(terms) == 1:
        return terms
    count = len(terms)
    even = eight_point(terms[0::2], sign)
    odd = eight_point(terms[1::2], sign)
    first, second = [], []
    for n in range(count // 2):
        re_part, im_part = odd[n]
        im_part = im_part if sign > 0 else -im_part
        turn = 8 * n // count
        if turn == 1:
            re_part, im_part = (re_part - im_part) * ROOT, (re_part + im_part) * ROOT
        elif turn == 2:
            re_part, im_part = -im_part, re_part
        elif turn == 3:
            re_part, im_part = -(re_part + im_part) * ROOT, (re_part - im_part) * ROOT
        im_part = im_part if sign > 0 else -im_part
        first.append((even[n][0] + re_part, even[n][1] + im_part))
        second.append((even[n][0] - re_part, even[n][1] - im_part))
    return first + second


def filter_kernel(rows_ref, spec_ref, table_ref, out_ref):
    lane = lane_ids(16) // 32
    blocks = []
    for col in range(NCOL):
        channels = []
        for channel in range(4):
            piece = jnp.zeros((16, 128), F32)
            for wave in range(NW):
                moved = pltpu.roll(rows_ref[col * NW + wave], (32 * (wave - channel)) % 128, 1)
                piece = jnp.where(lane == wave, moved, piece)
            channels.append(piece)
        blocks.append(
            (
                jnp.concatenate([channels[0], channels[2]], axis=0),
                jnp.concatenate([channels[1], channels[3]], axis=0),
            )
        )
    sums = eight_point(blocks, -1)
    scale = 1.0 / (NR * NC)
    back = []
    for n in range(8):
        operand = split(jnp.concatenate(sums[n], axis=0))
        mix = mm3(operand, (table_ref[0, n], table_ref[1, n]))
        freq_re = mix[:32, :128] + mix[32:, 128:]
        freq_im = mix[32:, :128] - mix[:32, 128:]
        image_re, known_re = freq_re[:16], freq_re[16:]
        image_im, known_im = freq_im[:16], freq_im[16:]
        spec_re, spec_im = spec_ref[n, 0:16], spec_ref[n, 16:32]
        blur_re = image_re * spec_re - image_im * spec_im
        blur_im = image_re * spec_im + image_im * spec_re
        rest_re = blur_re - known_re
        rest_im = blur_im - known_im
        pull_re = rest_re * spec_re + rest_im * spec_im
        pull_im = rest_im * spec_re - rest_re * spec_im
        both = jnp.concatenate([blur_re - pull_im, blur_im + pull_re], axis=0) * scale
        mix = mm3(split(both), (table_ref[2, n], table_ref[3, n]))
        back.append((mix[:16, :128] - mix[16:, 128:], mix[:16, 128:] + mix[16:, :128]))
    columns = eight_point(back, 1)
    for col in range(NCOL):
        left, right = edges(*columns[col])
        out_ref[col * NW + 1] = left
        out_ref[(col + 7) % 8 * NW + 3] = left
        out_ref[(col + 1) % 8 * NW] = right
        out_ref[col * NW + 2] = right


def halo_kernel(left_ref, right_ref, out_ref):
    for wave in range(LW):
        out_ref[0, wave], out_ref[1, wave] = halo_parts(left_ref[wave], right_ref[wave])


def row_inverse_kernel(rows_ref, table_ref, after_ref, out_ref):
    operand = split(rows_ref[...].reshape(NR, 128))
    mix = mm3((table_ref[0], table_ref[1]), operand)
    cos_part, sin_part = mix[:64], mix[64:]
    pulled = sin_part + swapped(cos_part)
    blurred = cos_part - swapped(sin_part)
    both = jnp.where(lane_ids(64) < 64, pulled, swapped(blurred))
    out_ref[...] = jnp.broadcast_to(both[None], out_ref.shape)


def back_columns_kernel(
    images_ref, measured_ref, field_ref, halo_ref, base_re_ref, base_im_ref,
    out_ref, residual_ref, centre_ref, border_ref, high_ref, low_ref,
):
    column_tables(base_re_ref, base_im_ref, high_ref, low_ref)
    low = lane_ids(64) < 64
    first, second = images_ref[1], images_ref[2]
    centre_ref[...] = jnp.where(low, first, swapped(second))
    residual_ref[...] = jnp.where(low, swapped(first), second) - measured_ref[...]
    border_ref[...] = jnp.where(low, images_ref[0], swapped(images_ref[3]))

    def step(wave):
        centre, border = centre_ref[...], border_ref[...]
        out_ref[0, wave], out_ref[1, wave] = column_pass(
            (field_ref[0, wave] * centre, halo_ref[0, wave] * border),
            (-field_ref[1, wave] * centre, -halo_ref[1, wave] * border),
            (high_ref[wave], low_ref[wave]),
        )

    over_waves(step)


def back_rows_kernel(
    weight_ref, up_ref, own_ref, down_ref, base_re_ref, base_im_ref, out_ref, high_ref, low_ref
):
    row_tables(base_re_ref, base_im_ref, high_ref, low_ref)

    def step(wave):
        re_out, im_out = row_pass(
            stacked_rows((up_ref, own_ref, down_ref), wave), (high_ref[wave], low_ref[wave])
        )
        factor = 2.0 * weight_ref[wave]
        out_ref[0, wave] = factor * re_out
        out_ref[1, wave] = -factor * im_out

    over_waves(step)


def params():
    return pltpu.CompilerParams(vmem_limit_bytes=VMEM_LIMIT)


def near(*dims, dtype=F32):
    return pltpu.VMEM(dims, dtype)


def far(*dims, dtype=F32):
    return pltpu.HBM(dims, dtype)


SMEM = pl.BlockSpec(memory_space=pltpu.SMEM)
ANY = pl.BlockSpec(memory_space=pl.ANY)
VM = pl.BlockSpec()


def kept(value):
    return pltpu.with_memory_space_constraint(value, pltpu.HBM)


def loaded(place, table):
    return pl.pallas_call(
        load_kernel,
        in_specs=[SMEM, ANY],
        out_shape=near(*table.shape[1:], dtype=BF16),
        scratch_shapes=[pltpu.SemaphoreType.DMA((1,))],
        compiler_params=params(),
    )(place, kept(jnp.asarray(table)))


def neighbours(value, axis, count, step):
    return lax.ppermute(
        value, axis, [(i, i + step) for i in range(count) if 0 <= i + step < count]
    )


def taps_of(wavelength):
    lane = jnp.arange(256)
    offset = jnp.where(lane < 128, lane, lane - 256).astype(F32)
    spread = jnp.arange(-HALO, HALO + 1).astype(F32)
    norm = 1.0 / jnp.sqrt(jnp.sum(jnp.exp(-2.0 * (spread / HALO) ** 2)))
    amplitude = jnp.where(jnp.abs(offset) <= HALO, jnp.exp(-((offset / HALO) ** 2)) * norm, 0.0)
    phase = offset * offset / (2.0 * wavelength[:, None] * HALO)
    return (amplitude * jnp.cos(phase))[:, None, :], (amplitude * jnp.sin(phase))[:, None, :]


def shards(wavefield, wavelength, weight, spectrum, measured):
    wave_place = lax.axis_index("wave")[None]
    row_place = lax.axis_index("row")[None]
    call = functools.partial(pl.pallas_call, compiler_params=params())
    field, edge, slots = (2, LW, 64, 128), (LW, 64, 128), (NCOL * NW, 16, 128)

    field_held, left_edge, right_edge = call(
        pack_kernel,
        in_specs=[ANY],
        out_shape=(near(*field), far(*edge), far(*edge)),
        scratch_shapes=[pltpu.SemaphoreType.DMA((LW,))],
    )(kept(wavefield))
    from_left = neighbours(right_edge, "col", NCOL, 1)
    from_right = neighbours(left_edge, "col", NCOL, -1)

    base = taps_of(wavelength)
    known_share, mirror, first = call(
        mirror_kernel,
        in_specs=[SMEM, ANY, ANY, ANY],
        out_shape=(near(48, 128), far(2, KB, 128), far(2, 8, 128)),
        scratch_shapes=[
            pltpu.VMEM((64, 128), F32), pltpu.VMEM((2, 64, 128), F32), pltpu.SemaphoreType.DMA((2,)),
        ],
    )(wave_place, kept(measured), kept(spectrum), kept(left_edge))
    mirror = lax.ppermute(mirror, "col", [(i, 7 - i) for i in range(NCOL)])
    first = lax.ppermute(first, "col", [(i, (8 - i) % 8) for i in range(NCOL)])
    known_share = call(share_kernel, in_specs=[SMEM, VM, VM, VM], out_shape=far(NROW, 80, 128))(
        wave_place, known_share, mirror, first
    )
    known = known_share
    known = lax.all_to_all(known, "row", split_axis=0, concat_axis=0, tiled=True)
    spec = call(order_kernel, out_shape=near(8, 32, 128))(
        known, jnp.asarray(column_order()), jnp.asarray(np.eye(128)[::-1].astype(ml_dtypes.bfloat16))
    )

    col_scratch = [pltpu.VMEM((LW, 256, 256), BF16)] * 2
    row_scratch = [pltpu.VMEM((LW, 128, 192), BF16)] * 2
    middle = call(
        columns_kernel,
        in_specs=[VM] * 5 + [ANY],
        out_shape=near(*field),
        scratch_shapes=col_scratch,
    )(field_held, from_left, from_right, *base, kept(known_share))
    from_up = neighbours(middle, "row", NROW, 1)
    from_down = neighbours(middle, "row", NROW, -1)
    propagated, left_edge, right_edge, shares = call(
        rows_kernel,
        in_specs=[SMEM] + [VM] * 5,
        out_shape=(near(*field), far(*edge), far(*edge), far(*slots)),
        scratch_shapes=[pltpu.VMEM((64, 128), F32)] + row_scratch,
    )(weight, from_up, middle, from_down, *base)

    prop_left = neighbours(right_edge, "col", NCOL, 1)
    prop_right = neighbours(left_edge, "col", NCOL, -1)
    prop_halo = call(
        halo_kernel,
        out_shape=near(*field),
        cost_estimate=pl.CostEstimate(flops=0, bytes_accessed=HALO_BYTES, transcendentals=0),
    )(prop_left, prop_right)

    image = lax.all_to_all(shares, ("wave", "row"), split_axis=0, concat_axis=0, tiled=True)
    first_place = jnp.zeros((1,), jnp.int32)
    row_dft = loaded(first_place, np.stack(row_dft_table())[None])
    freq_rows = call(row_dft_kernel, out_shape=far(*slots))(image, known, row_dft)
    freq_rows = lax.all_to_all(freq_rows, ("col", "wave"), split_axis=0, concat_axis=0, tiled=True)

    col_dft = loaded(first_place, np.stack(col_dft_table() + col_inverse_table())[None])
    columns = call(filter_kernel, out_shape=far(*slots))(freq_rows, spec, col_dft)
    columns = lax.all_to_all(columns, ("col", "wave"), split_axis=0, concat_axis=0, tiled=True)

    row_back = loaded(row_place, np.stack(row_inverse_table(), axis=1))
    images = call(row_inverse_kernel, in_specs=[VM, VM, ANY], out_shape=far(NW, 64, 128))(
        columns, row_back, prop_halo
    )
    images = lax.all_to_all(images, "wave", split_axis=0, concat_axis=0, tiled=True)

    middle, residual = call(
        back_columns_kernel,
        out_shape=(near(*field), far(64, 128)),
        scratch_shapes=[pltpu.VMEM((64, 128), F32)] * 2 + col_scratch,
    )(images, measured, propagated, prop_halo, *base)
    from_up = neighbours(middle, "row", NROW, 1)
    from_down = neighbours(middle, "row", NROW, -1)
    field_grad = call(
        back_rows_kernel,
        in_specs=[SMEM] + [VM] * 5,
        out_shape=far(*field),
        scratch_shapes=row_scratch,
    )(weight, from_up, middle, from_down, *base)
    return field_grad, residual


def solution(mesh):
    placed = (
        P(None, "wave", "row", "col"),
        P("wave"),
        P("wave"),
        P(None, "col", "row"),
        P("row", "col"),
    )
    return jax.shard_map(
        shards,
        mesh=mesh,
        in_specs=placed,
        out_specs=(P(None, "wave", "row", "col"), P("row", "col")),
        check_vma=False,
    )
```

```python
import functools

import jax
import jax.numpy as jnp
import ml_dtypes
import numpy as np
from jax import lax
from jax.experimental import pallas as pl
from jax.experimental.pallas import tpu as pltpu
from jax.sharding import PartitionSpec as P

WAVES = 32
HALO = 64
TR = 64
TC = 128
NR = 512
NC = 1024
NW = 4
NROW = 8
NCOL = 8
LW = WAVES // NW
QC = TC // NW
KB = NR // (NCOL * NW)
STEP = 2
LONG = pl.CostEstimate(flops=1 << 50, bytes_accessed=1 << 36, transcendentals=1 << 40)
ROOT = float(np.sqrt(0.5))
F32 = jnp.float32
BF16 = jnp.bfloat16
VMEM_LIMIT = 20 * 1024 * 1024


def halves_of(table):
    high = table.astype(ml_dtypes.bfloat16)
    low = (table - high.astype(np.float64)).astype(ml_dtypes.bfloat16)
    return high, low


@functools.lru_cache(None)
def row_dft_table():
    group, block, inner = np.meshgrid(np.arange(4), np.arange(NROW), np.arange(16), indexing="ij")
    rows = (TR * block + 16 * group + inner).reshape(-1)
    angle = 2 * np.pi * (np.arange(NR)[:, None] * rows[None, :] % NR) / NR
    return halves_of(np.concatenate([np.cos(angle), -np.sin(angle)], axis=1))


@functools.lru_cache(None)
def col_dft_table():
    freq = (8 * np.arange(128)[None, :] + np.arange(8)[:, None])[:, None, :]
    angle = 2 * np.pi * (np.arange(128)[None, :, None] * freq % NC) / NC
    return halves_of(np.concatenate([np.cos(angle), np.sin(angle)], axis=2))


@functools.lru_cache(None)
def col_inverse_table():
    freq = (8 * np.arange(128)[None, :] + np.arange(8)[:, None])[:, :, None]
    angle = 2 * np.pi * (np.arange(128)[None, None, :] * freq % NC) / NC
    return halves_of(np.concatenate([np.cos(angle), np.sin(angle)], axis=2))


@functools.lru_cache(None)
def column_order():
    table = np.zeros((128, 128))
    for m in range(16):
        for n in range(8):
            table[8 * m + n, 16 * n + m] = 1.0
    return table.astype(ml_dtypes.bfloat16)


@functools.lru_cache(None)
def row_inverse_table():
    rows = TR * np.arange(NROW)[:, None] + np.arange(TR)[None, :]
    angle = 2 * np.pi * (rows[:, :, None] * np.arange(NR)[None, None, :] % NR) / NR
    return halves_of(np.concatenate([np.cos(angle), np.sin(angle)], axis=1))


def split(values):
    high = values.astype(BF16)
    return high, (values - high.astype(F32)).astype(BF16)


def mm(left, right):
    return jnp.dot(left, right, preferred_element_type=F32)


def mm3(left, right):
    rows = left[0].shape[0]
    most = mm(jnp.concatenate(left, axis=0), right[0])
    return most[:rows] + (most[rows:] + mm(left[0], right[1]))


def three(values):
    high = values.astype(BF16)
    middle, low = split(values - high.astype(F32))
    return high, middle, low


def lane_ids(rows, lanes=128):
    return lax.broadcasted_iota(jnp.int32, (rows, lanes), 1)


def swapped(values):
    return pltpu.roll(values, 64, 1)


def column_taps(base):
    wide = jnp.broadcast_to(base, (128, 256))
    own = pltpu.roll(wide, 0, 1, stride=1, stride_axis=0)[:, :128]
    left = pltpu.roll(wide[:64], 256 - 64, 1, stride=1, stride_axis=0)[:, :128]
    right = pltpu.roll(wide[:64], 128, 1, stride=1, stride_axis=0)[:, :128]
    return jnp.concatenate([own, left, right], axis=0)


def row_taps(base):
    wide = jnp.broadcast_to(base, (64, 256))
    return pltpu.roll(wide, 64, 1, stride=1, stride_axis=0)[:, :192]


def column_pass(parts_re, parts_im, table):
    rows = parts_re[0].shape[0]
    field = jnp.concatenate(
        [jnp.concatenate(parts_re, axis=1), jnp.concatenate(parts_im, axis=1)], axis=0
    )
    mix = mm3(split(field), table)
    return (
        mix[:rows, :128] - mix[rows:, 128:],
        mix[:rows, 128:] + mix[rows:, :128],
    )


def row_pass(stacked, table):
    mix = mm3(table, split(stacked))
    return mix[:64, :128] - mix[64:, 128:], mix[:64, 128:] + mix[64:, :128]


def over_waves(step):
    def body(start, carry):
        for wave in range(STEP):
            step(start * STEP + wave)
        return carry

    lax.fori_loop(0, LW // STEP, body, 0)


def edges(re_part, im_part):
    lane = lane_ids(re_part.shape[0])
    return (
        jnp.where(lane < 64, re_part, swapped(im_part)),
        jnp.where(lane < 64, swapped(re_part), im_part),
    )


def halo_parts(from_left, from_right):
    lane = lane_ids(from_left.shape[0])
    return (
        jnp.where(lane < 64, from_left, swapped(from_right)),
        jnp.where(lane < 64, swapped(from_left), from_right),
    )


def quarter(block, which):
    lane = lane_ids(16)
    out = jnp.zeros((16, 128), F32)
    for group in range(4):
        amount = lax.rem(32 * group - 32 * which + 128, 128)
        moved = pltpu.roll(block[16 * group : 16 * group + 16], amount, 1)
        out = jnp.where(lane // 32 == group, moved, out)
    return out


def fetch(pairs, sems):
    copies = [
        pltpu.make_async_copy(source, target, sems.at[i])
        for i, (source, target) in enumerate(pairs)
    ]
    for copy in copies:
        copy.start()
    return copies


def load_kernel(place_ref, table_ref, out_ref, sems):
    for copy in fetch([(table_ref.at[place_ref[0]], out_ref)], sems):
        copy.wait()


def pack_kernel(field_ref, held_ref, left_ref, right_ref, sems):
    copies = fetch([(field_ref.at[:, wave], held_ref.at[:, wave]) for wave in range(LW)], sems)
    for wave in range(LW):
        copies[wave].wait()
        left, right = edges(held_ref[0, wave], held_ref[1, wave])
        left_ref[wave] = left
        right_ref[wave] = right


def mirror_kernel(
    place_ref, measured_ref, spec_ref, after_ref, share_ref, mirror_ref, first_ref,
    measured_in, spec_in, sems,
):
    copies = fetch([(spec_ref, spec_in), (measured_ref, measured_in)], sems)
    place = place_ref[0]
    row = lax.broadcasted_iota(jnp.int32, (16, 64), 0)
    pick = (lane_ids(16, 64) == 64 - KB * place - row).astype(BF16)
    copies[0].wait()
    start = pl.multiple_of(place * KB, KB)
    for part in range(2):
        mirror_ref[part] = sum(mm(pick, piece) for piece in three(spec_in[part]))
        first_ref[part] = spec_in[part, 0:8]
        share_ref[16 + 16 * part : 32 + 16 * part] = spec_in[part, pl.ds(start, KB)]
    copies[1].wait()
    share_ref[0:16] = quarter(measured_in[...], place)


def share_kernel(place_ref, share_ref, mirror_ref, first_ref, out_ref):
    place = place_ref[0]
    top = lax.broadcasted_iota(jnp.int32, (16, 128), 0) == 0
    rows = [share_ref[...]]
    for part in range(2):
        other = jnp.broadcast_to(first_ref[part, 0:1], (16, 128))
        rows.append(jnp.where(jnp.logical_and(top, place == 0), other, mirror_ref[part]))
    out_ref[...] = jnp.broadcast_to(jnp.concatenate(rows, axis=0)[None], out_ref.shape)


def order_kernel(rows_ref, order_ref, reverse_ref, out_ref):
    order, reverse = order_ref[...], reverse_ref[...]
    lane = lane_ids(64) // 16
    parts = []
    for row in range(NROW):
        parts.append(sum(mm(piece, order) for piece in three(rows_ref[row, 16:80])))
    ordered = []
    for n in range(8):
        out = jnp.zeros((64, 128), F32)
        for row in range(NROW):
            moved = pltpu.roll(parts[row], (16 * (row - n)) % 128, 1)
            out = jnp.where(lane == row, moved, out)
        ordered.append(out)
    for n in range(8):
        back = sum(mm(piece, reverse) for piece in three(ordered[(8 - n) % 8][32:]))
        if n == 0:
            back = pltpu.roll(back, 1, 1)
        out_ref[n, 0:16] = 0.5 * (ordered[n][0:16] + back[0:16])
        out_ref[n, 16:32] = 0.5 * (ordered[n][16:32] - back[16:32])


def column_tables(base_re_ref, base_im_ref, high_ref, low_ref):
    for wave in range(LW):
        high_ref[wave], low_ref[wave] = split(
            jnp.concatenate(
                [column_taps(base_re_ref[wave]), column_taps(base_im_ref[wave])], axis=1
            )
        )


def row_tables(base_re_ref, base_im_ref, high_ref, low_ref):
    for wave in range(LW):
        high_ref[wave], low_ref[wave] = split(
            jnp.concatenate([row_taps(base_re_ref[wave]), row_taps(base_im_ref[wave])], axis=0)
        )


def columns_kernel(
    field_ref, left_ref, right_ref, base_re_ref, base_im_ref, after_ref, out_ref, high_ref, low_ref
):
    column_tables(base_re_ref, base_im_ref, high_ref, low_ref)

    def step(wave):
        halo_re, halo_im = halo_parts(left_ref[wave], right_ref[wave])
        out_ref[0, wave], out_ref[1, wave] = column_pass(
            (field_ref[0, wave], halo_re),
            (field_ref[1, wave], halo_im),
            (high_ref[wave], low_ref[wave]),
        )

    over_waves(step)


def stacked_rows(refs, wave):
    return jnp.concatenate(
        [jnp.concatenate([ref[0, wave], ref[1, wave]], axis=1) for ref in refs], axis=0
    )


def rows_kernel(
    weight_ref, up_ref, own_ref, down_ref, base_re_ref, base_im_ref,
    out_ref, left_ref, right_ref, share_ref, total_ref, high_ref, low_ref,
):
    row_tables(base_re_ref, base_im_ref, high_ref, low_ref)
    total_ref[...] = jnp.zeros_like(total_ref)

    def step(wave):
        re_out, im_out = row_pass(
            stacked_rows((up_ref, own_ref, down_ref), wave), (high_ref[wave], low_ref[wave])
        )
        out_ref[0, wave] = re_out
        out_ref[1, wave] = im_out
        left, right = edges(re_out, im_out)
        left_ref[wave] = left
        right_ref[wave] = right
        total_ref[...] += weight_ref[wave] * (re_out * re_out + im_out * im_out)

    over_waves(step)
    block = total_ref[...] * (1.0 / WAVES)
    for target in range(NW):
        piece = quarter(block, target)
        share_ref[target * NROW : (target + 1) * NROW] = jnp.broadcast_to(
            piece[None], (NROW, 16, 128)
        )


def row_dft_kernel(image_ref, measured_ref, table_ref, out_ref):
    summed = image_ref[0:NROW] + image_ref[NROW : 2 * NROW]
    summed = summed + image_ref[2 * NROW : 3 * NROW]
    summed = (summed + image_ref[3 * NROW : 4 * NROW]).reshape(128, 128)
    known = measured_ref[:, 0:16].reshape(128, 128)
    lane = lane_ids(128) // 32
    top = []
    low = []
    for group in range(4):
        first = pltpu.roll(summed, (128 - 32 * group) % 128, 1)
        third = pltpu.roll(known, (192 - 32 * group) % 128, 1)
        both = jnp.where(lane == 0, first, jnp.where(lane == 2, third, 0.0))
        top.append(both)
        low.append(pltpu.roll(both, 32, 1))
    operand = split(jnp.concatenate(top + low, axis=0))
    out_ref[...] = mm3((table_ref[0], table_ref[1]), operand).reshape(out_ref.shape)


def eight_point(terms, sign):
    if len(terms) == 1:
        return terms
    count = len(terms)
    even = eight_point(terms[0::2], sign)
    odd = eight_point(terms[1::2], sign)
    first, second = [], []
    for n in range(count // 2):
        re_part, im_part = odd[n]
        im_part = im_part if sign > 0 else -im_part
        turn = 8 * n // count
        if turn == 1:
            re_part, im_part = (re_part - im_part) * ROOT, (re_part + im_part) * ROOT
        elif turn == 2:
            re_part, im_part = -im_part, re_part
        elif turn == 3:
            re_part, im_part = -(re_part + im_part) * ROOT, (re_part - im_part) * ROOT
        im_part = im_part if sign > 0 else -im_part
        first.append((even[n][0] + re_part, even[n][1] + im_part))
        second.append((even[n][0] - re_part, even[n][1] - im_part))
    return first + second


def filter_kernel(rows_ref, spec_ref, table_ref, out_ref):
    lane = lane_ids(16) // 32
    blocks = []
    for col in range(NCOL):
        channels = []
        for channel in range(4):
            piece = jnp.zeros((16, 128), F32)
            for wave in range(NW):
                moved = pltpu.roll(rows_ref[col * NW + wave], (32 * (wave - channel)) % 128, 1)
                piece = jnp.where(lane == wave, moved, piece)
            channels.append(piece)
        blocks.append(
            (
                jnp.concatenate([channels[0], channels[2]], axis=0),
                jnp.concatenate([channels[1], channels[3]], axis=0),
            )
        )
    sums = eight_point(blocks, -1)
    scale = 1.0 / (NR * NC)
    back = []
    for n in range(8):
        operand = split(jnp.concatenate(sums[n], axis=0))
        mix = mm3(operand, (table_ref[0, n], table_ref[1, n]))
        freq_re = mix[:32, :128] + mix[32:, 128:]
        freq_im = mix[32:, :128] - mix[:32, 128:]
        image_re, known_re = freq_re[:16], freq_re[16:]
        image_im, known_im = freq_im[:16], freq_im[16:]
        spec_re, spec_im = spec_ref[n, 0:16], spec_ref[n, 16:32]
        blur_re = image_re * spec_re - image_im * spec_im
        blur_im = image_re * spec_im + image_im * spec_re
        rest_re = blur_re - known_re
        rest_im = blur_im - known_im
        pull_re = rest_re * spec_re + rest_im * spec_im
        pull_im = rest_im * spec_re - rest_re * spec_im
        both = jnp.concatenate([blur_re - pull_im, blur_im + pull_re], axis=0) * scale
        mix = mm3(split(both), (table_ref[2, n], table_ref[3, n]))
        back.append((mix[:16, :128] - mix[16:, 128:], mix[:16, 128:] + mix[16:, :128]))
    columns = eight_point(back, 1)
    for col in range(NCOL):
        left, right = edges(*columns[col])
        out_ref[col * NW + 1] = left
        out_ref[(col + 7) % 8 * NW + 3] = left
        out_ref[(col + 1) % 8 * NW] = right
        out_ref[col * NW + 2] = right


def halo_kernel(left_ref, right_ref, out_ref):
    for wave in range(LW):
        out_ref[0, wave], out_ref[1, wave] = halo_parts(left_ref[wave], right_ref[wave])


def row_inverse_kernel(rows_ref, table_ref, out_ref):
    operand = split(rows_ref[...].reshape(NR, 128))
    mix = mm3((table_ref[0], table_ref[1]), operand)
    cos_part, sin_part = mix[:64], mix[64:]
    pulled = sin_part + swapped(cos_part)
    blurred = cos_part - swapped(sin_part)
    both = jnp.where(lane_ids(64) < 64, pulled, swapped(blurred))
    out_ref[...] = jnp.broadcast_to(both[None], out_ref.shape)


def back_columns_kernel(
    images_ref, measured_ref, field_ref, halo_ref, base_re_ref, base_im_ref,
    out_ref, residual_ref, centre_ref, border_ref, high_ref, low_ref,
):
    column_tables(base_re_ref, base_im_ref, high_ref, low_ref)
    low = lane_ids(64) < 64
    first, second = images_ref[1], images_ref[2]
    centre_ref[...] = jnp.where(low, first, swapped(second))
    residual_ref[...] = jnp.where(low, swapped(first), second) - measured_ref[...]
    border_ref[...] = jnp.where(low, images_ref[0], swapped(images_ref[3]))

    def step(wave):
        centre, border = centre_ref[...], border_ref[...]
        out_ref[0, wave], out_ref[1, wave] = column_pass(
            (field_ref[0, wave] * centre, halo_ref[0, wave] * border),
            (-field_ref[1, wave] * centre, -halo_ref[1, wave] * border),
            (high_ref[wave], low_ref[wave]),
        )

    over_waves(step)


def back_rows_kernel(
    weight_ref, up_ref, own_ref, down_ref, base_re_ref, base_im_ref, out_ref, high_ref, low_ref
):
    row_tables(base_re_ref, base_im_ref, high_ref, low_ref)

    def step(wave):
        re_out, im_out = row_pass(
            stacked_rows((up_ref, own_ref, down_ref), wave), (high_ref[wave], low_ref[wave])
        )
        factor = 2.0 * weight_ref[wave]
        out_ref[0, wave] = factor * re_out
        out_ref[1, wave] = -factor * im_out

    over_waves(step)


def params():
    return pltpu.CompilerParams(vmem_limit_bytes=VMEM_LIMIT)


def near(*dims, dtype=F32):
    return pltpu.VMEM(dims, dtype)


def far(*dims, dtype=F32):
    return pltpu.HBM(dims, dtype)


SMEM = pl.BlockSpec(memory_space=pltpu.SMEM)
ANY = pl.BlockSpec(memory_space=pl.ANY)
VM = pl.BlockSpec()


def kept(value):
    return pltpu.with_memory_space_constraint(value, pltpu.HBM)


def loaded(place, table):
    return pl.pallas_call(
        load_kernel,
        in_specs=[SMEM, ANY],
        out_shape=near(*table.shape[1:], dtype=BF16),
        scratch_shapes=[pltpu.SemaphoreType.DMA((1,))],
        compiler_params=params(),
    )(place, kept(jnp.asarray(table)))


def neighbours(value, axis, count, step):
    return lax.ppermute(
        value, axis, [(i, i + step) for i in range(count) if 0 <= i + step < count]
    )


def taps_of(wavelength):
    lane = jnp.arange(256)
    offset = jnp.where(lane < 128, lane, lane - 256).astype(F32)
    spread = jnp.arange(-HALO, HALO + 1).astype(F32)
    norm = 1.0 / jnp.sqrt(jnp.sum(jnp.exp(-2.0 * (spread / HALO) ** 2)))
    amplitude = jnp.where(jnp.abs(offset) <= HALO, jnp.exp(-((offset / HALO) ** 2)) * norm, 0.0)
    phase = offset * offset / (2.0 * wavelength[:, None] * HALO)
    return (amplitude * jnp.cos(phase))[:, None, :], (amplitude * jnp.sin(phase))[:, None, :]


def shards(wavefield, wavelength, weight, spectrum, measured):
    wave_place = lax.axis_index("wave")[None]
    row_place = lax.axis_index("row")[None]
    call = functools.partial(pl.pallas_call, compiler_params=params())
    field, edge, slots = (2, LW, 64, 128), (LW, 64, 128), (NCOL * NW, 16, 128)

    field_held, left_edge, right_edge = call(
        pack_kernel,
        in_specs=[ANY],
        out_shape=(near(*field), far(*edge), far(*edge)),
        scratch_shapes=[pltpu.SemaphoreType.DMA((LW,))],
    )(kept(wavefield))
    from_left = neighbours(right_edge, "col", NCOL, 1)
    from_right = neighbours(left_edge, "col", NCOL, -1)

    base = taps_of(wavelength)
    known_share, mirror, first = call(
        mirror_kernel,
        in_specs=[SMEM, ANY, ANY, ANY],
        out_shape=(near(48, 128), far(2, KB, 128), far(2, 8, 128)),
        scratch_shapes=[
            pltpu.VMEM((64, 128), F32), pltpu.VMEM((2, 64, 128), F32), pltpu.SemaphoreType.DMA((2,)),
        ],
    )(wave_place, kept(measured), kept(spectrum), kept(left_edge))
    mirror = lax.ppermute(mirror, "col", [(i, 7 - i) for i in range(NCOL)])
    first = lax.ppermute(first, "col", [(i, (8 - i) % 8) for i in range(NCOL)])
    known_share = call(share_kernel, in_specs=[SMEM, VM, VM, VM], out_shape=far(NROW, 80, 128))(
        wave_place, known_share, mirror, first
    )
    known = known_share
    known = lax.all_to_all(known, "row", split_axis=0, concat_axis=0, tiled=True)
    spec = call(order_kernel, out_shape=near(8, 32, 128))(
        known, jnp.asarray(column_order()), jnp.asarray(np.eye(128)[::-1].astype(ml_dtypes.bfloat16))
    )

    col_scratch = [pltpu.VMEM((LW, 256, 256), BF16)] * 2
    row_scratch = [pltpu.VMEM((LW, 128, 192), BF16)] * 2
    middle = call(
        columns_kernel,
        in_specs=[VM] * 5 + [ANY],
        out_shape=near(*field),
        scratch_shapes=col_scratch,
    )(field_held, from_left, from_right, *base, kept(known_share))
    from_up = neighbours(middle, "row", NROW, 1)
    from_down = neighbours(middle, "row", NROW, -1)
    propagated, left_edge, right_edge, shares = call(
        rows_kernel,
        in_specs=[SMEM] + [VM] * 5,
        out_shape=(near(*field), far(*edge), far(*edge), far(*slots)),
        scratch_shapes=[pltpu.VMEM((64, 128), F32)] + row_scratch,
    )(weight, from_up, middle, from_down, *base)

    prop_left = neighbours(right_edge, "col", NCOL, 1)
    prop_right = neighbours(left_edge, "col", NCOL, -1)
    prop_halo = call(
        halo_kernel,
        out_shape=near(*field),
        cost_estimate=LONG,
    )(prop_left, prop_right)

    image = lax.all_to_all(shares, ("wave", "row"), split_axis=0, concat_axis=0, tiled=True)
    first_place = jnp.zeros((1,), jnp.int32)
    row_dft = loaded(first_place, np.stack(row_dft_table())[None])
    freq_rows = call(row_dft_kernel, out_shape=far(*slots))(image, known, row_dft)
    freq_rows = lax.all_to_all(freq_rows, ("col", "wave"), split_axis=0, concat_axis=0, tiled=True)

    col_dft = loaded(first_place, np.stack(col_dft_table() + col_inverse_table())[None])
    columns = call(filter_kernel, out_shape=far(*slots))(freq_rows, spec, col_dft)
    columns = lax.all_to_all(columns, ("col", "wave"), split_axis=0, concat_axis=0, tiled=True)

    row_back = loaded(row_place, np.stack(row_inverse_table(), axis=1))
    images = call(row_inverse_kernel, out_shape=far(NW, 64, 128))(columns, row_back)
    images = lax.all_to_all(images, "wave", split_axis=0, concat_axis=0, tiled=True)

    middle, residual = call(
        back_columns_kernel,
        out_shape=(near(*field), far(64, 128)),
        scratch_shapes=[pltpu.VMEM((64, 128), F32)] * 2 + col_scratch,
    )(images, measured, propagated, prop_halo, *base)
    from_up = neighbours(middle, "row", NROW, 1)
    from_down = neighbours(middle, "row", NROW, -1)
    field_grad = call(
        back_rows_kernel,
        in_specs=[SMEM] + [VM] * 5,
        out_shape=far(*field),
        scratch_shapes=row_scratch,
    )(weight, from_up, middle, from_down, *base)
    return field_grad, residual


def solution(mesh):
    placed = (
        P(None, "wave", "row", "col"),
        P("wave"),
        P("wave"),
        P(None, "col", "row"),
        P("row", "col"),
    )
    return jax.shard_map(
        shards,
        mesh=mesh,
        in_specs=placed,
        out_specs=(P(None, "wave", "row", "col"), P("row", "col")),
        check_vma=False,
    )
```

```python
import functools

import jax
import jax.numpy as jnp
import ml_dtypes
import numpy as np
from jax import lax
from jax.experimental import pallas as pl
from jax.experimental.pallas import tpu as pltpu
from jax.sharding import PartitionSpec as P

WAVES = 32
HALO = 64
TR = 64
TC = 128
NR = 512
NC = 1024
NW = 4
NROW = 8
NCOL = 8
LW = WAVES // NW
QC = TC // NW
KB = NR // (NCOL * NW)
STEP = 2
MEDIUM = pl.CostEstimate(flops=1 << 36, bytes_accessed=0, transcendentals=0)
ROOT = float(np.sqrt(0.5))
F32 = jnp.float32
BF16 = jnp.bfloat16
VMEM_LIMIT = 20 * 1024 * 1024


def halves_of(table):
    high = table.astype(ml_dtypes.bfloat16)
    low = (table - high.astype(np.float64)).astype(ml_dtypes.bfloat16)
    return high, low


@functools.lru_cache(None)
def row_dft_table():
    group, block, inner = np.meshgrid(np.arange(4), np.arange(NROW), np.arange(16), indexing="ij")
    rows = (TR * block + 16 * group + inner).reshape(-1)
    angle = 2 * np.pi * (np.arange(NR)[:, None] * rows[None, :] % NR) / NR
    return halves_of(np.concatenate([np.cos(angle), -np.sin(angle)], axis=1))


@functools.lru_cache(None)
def col_dft_table():
    freq = (8 * np.arange(128)[None, :] + np.arange(8)[:, None])[:, None, :]
    angle = 2 * np.pi * (np.arange(128)[None, :, None] * freq % NC) / NC
    return halves_of(np.concatenate([np.cos(angle), np.sin(angle)], axis=2))


@functools.lru_cache(None)
def col_inverse_table():
    freq = (8 * np.arange(128)[None, :] + np.arange(8)[:, None])[:, :, None]
    angle = 2 * np.pi * (np.arange(128)[None, None, :] * freq % NC) / NC
    return halves_of(np.concatenate([np.cos(angle), np.sin(angle)], axis=2))


@functools.lru_cache(None)
def column_order():
    table = np.zeros((128, 128))
    for m in range(16):
        for n in range(8):
            table[8 * m + n, 16 * n + m] = 1.0
    return table.astype(ml_dtypes.bfloat16)


@functools.lru_cache(None)
def row_inverse_table():
    rows = TR * np.arange(NROW)[:, None] + np.arange(TR)[None, :]
    angle = 2 * np.pi * (rows[:, :, None] * np.arange(NR)[None, None, :] % NR) / NR
    return halves_of(np.concatenate([np.cos(angle), np.sin(angle)], axis=1))


def split(values):
    high = values.astype(BF16)
    return high, (values - high.astype(F32)).astype(BF16)


def mm(left, right):
    return jnp.dot(left, right, preferred_element_type=F32)


def mm3(left, right):
    rows = left[0].shape[0]
    most = mm(jnp.concatenate(left, axis=0), right[0])
    return most[:rows] + (most[rows:] + mm(left[0], right[1]))


def three(values):
    high = values.astype(BF16)
    middle, low = split(values - high.astype(F32))
    return high, middle, low


def lane_ids(rows, lanes=128):
    return lax.broadcasted_iota(jnp.int32, (rows, lanes), 1)


def swapped(values):
    return pltpu.roll(values, 64, 1)


def column_taps(base):
    wide = jnp.broadcast_to(base, (128, 256))
    own = pltpu.roll(wide, 0, 1, stride=1, stride_axis=0)[:, :128]
    left = pltpu.roll(wide[:64], 256 - 64, 1, stride=1, stride_axis=0)[:, :128]
    right = pltpu.roll(wide[:64], 128, 1, stride=1, stride_axis=0)[:, :128]
    return jnp.concatenate([own, left, right], axis=0)


def row_taps(base):
    wide = jnp.broadcast_to(base, (64, 256))
    return pltpu.roll(wide, 64, 1, stride=1, stride_axis=0)[:, :192]


def column_pass(parts_re, parts_im, table):
    rows = parts_re[0].shape[0]
    field = jnp.concatenate(
        [jnp.concatenate(parts_re, axis=1), jnp.concatenate(parts_im, axis=1)], axis=0
    )
    mix = mm3(split(field), table)
    return (
        mix[:rows, :128] - mix[rows:, 128:],
        mix[:rows, 128:] + mix[rows:, :128],
    )


def row_pass(stacked, table):
    mix = mm3(table, split(stacked))
    return mix[:64, :128] - mix[64:, 128:], mix[:64, 128:] + mix[64:, :128]


def over_waves(step):
    def body(start, carry):
        for wave in range(STEP):
            step(start * STEP + wave)
        return carry

    lax.fori_loop(0, LW // STEP, body, 0)


def edges(re_part, im_part):
    lane = lane_ids(re_part.shape[0])
    return (
        jnp.where(lane < 64, re_part, swapped(im_part)),
        jnp.where(lane < 64, swapped(re_part), im_part),
    )


def halo_parts(from_left, from_right):
    lane = lane_ids(from_left.shape[0])
    return (
        jnp.where(lane < 64, from_left, swapped(from_right)),
        jnp.where(lane < 64, swapped(from_left), from_right),
    )


def quarter(block, which):
    lane = lane_ids(16)
    out = jnp.zeros((16, 128), F32)
    for group in range(4):
        amount = lax.rem(32 * group - 32 * which + 128, 128)
        moved = pltpu.roll(block[16 * group : 16 * group + 16], amount, 1)
        out = jnp.where(lane // 32 == group, moved, out)
    return out


def fetch(pairs, sems):
    copies = [
        pltpu.make_async_copy(source, target, sems.at[i])
        for i, (source, target) in enumerate(pairs)
    ]
    for copy in copies:
        copy.start()
    return copies


def load_kernel(place_ref, table_ref, out_ref, sems):
    for copy in fetch([(table_ref.at[place_ref[0]], out_ref)], sems):
        copy.wait()


def pack_kernel(field_ref, held_ref, left_ref, right_ref, sems):
    copies = fetch([(field_ref.at[:, wave], held_ref.at[:, wave]) for wave in range(LW)], sems)
    for wave in range(LW):
        copies[wave].wait()
        left, right = edges(held_ref[0, wave], held_ref[1, wave])
        left_ref[wave] = left
        right_ref[wave] = right


def mirror_kernel(
    place_ref, measured_ref, spec_ref, after_ref, share_ref, mirror_ref, first_ref,
    measured_in, spec_in, sems,
):
    copies = fetch([(spec_ref, spec_in), (measured_ref, measured_in)], sems)
    place = place_ref[0]
    row = lax.broadcasted_iota(jnp.int32, (16, 64), 0)
    pick = (lane_ids(16, 64) == 64 - KB * place - row).astype(BF16)
    copies[0].wait()
    start = pl.multiple_of(place * KB, KB)
    for part in range(2):
        mirror_ref[part] = sum(mm(pick, piece) for piece in three(spec_in[part]))
        first_ref[part] = spec_in[part, 0:8]
        share_ref[16 + 16 * part : 32 + 16 * part] = spec_in[part, pl.ds(start, KB)]
    copies[1].wait()
    share_ref[0:16] = quarter(measured_in[...], place)


def share_kernel(place_ref, share_ref, mirror_ref, first_ref, out_ref):
    place = place_ref[0]
    top = lax.broadcasted_iota(jnp.int32, (16, 128), 0) == 0
    rows = [share_ref[...]]
    for part in range(2):
        other = jnp.broadcast_to(first_ref[part, 0:1], (16, 128))
        rows.append(jnp.where(jnp.logical_and(top, place == 0), other, mirror_ref[part]))
    out_ref[...] = jnp.broadcast_to(jnp.concatenate(rows, axis=0)[None], out_ref.shape)


def order_kernel(rows_ref, order_ref, reverse_ref, out_ref):
    order, reverse = order_ref[...], reverse_ref[...]
    lane = lane_ids(64) // 16
    parts = []
    for row in range(NROW):
        parts.append(sum(mm(piece, order) for piece in three(rows_ref[row, 16:80])))
    ordered = []
    for n in range(8):
        out = jnp.zeros((64, 128), F32)
        for row in range(NROW):
            moved = pltpu.roll(parts[row], (16 * (row - n)) % 128, 1)
            out = jnp.where(lane == row, moved, out)
        ordered.append(out)
    for n in range(8):
        back = sum(mm(piece, reverse) for piece in three(ordered[(8 - n) % 8][32:]))
        if n == 0:
            back = pltpu.roll(back, 1, 1)
        out_ref[n, 0:16] = 0.5 * (ordered[n][0:16] + back[0:16])
        out_ref[n, 16:32] = 0.5 * (ordered[n][16:32] - back[16:32])


def column_tables(base_re_ref, base_im_ref, high_ref, low_ref):
    for wave in range(LW):
        high_ref[wave], low_ref[wave] = split(
            jnp.concatenate(
                [column_taps(base_re_ref[wave]), column_taps(base_im_ref[wave])], axis=1
            )
        )


def row_tables(base_re_ref, base_im_ref, high_ref, low_ref):
    for wave in range(LW):
        high_ref[wave], low_ref[wave] = split(
            jnp.concatenate([row_taps(base_re_ref[wave]), row_taps(base_im_ref[wave])], axis=0)
        )


def columns_kernel(
    field_ref, left_ref, right_ref, base_re_ref, base_im_ref, after_ref, out_ref, high_ref, low_ref
):
    column_tables(base_re_ref, base_im_ref, high_ref, low_ref)

    def step(wave):
        halo_re, halo_im = halo_parts(left_ref[wave], right_ref[wave])
        out_ref[0, wave], out_ref[1, wave] = column_pass(
            (field_ref[0, wave], halo_re),
            (field_ref[1, wave], halo_im),
            (high_ref[wave], low_ref[wave]),
        )

    over_waves(step)


def stacked_rows(refs, wave):
    return jnp.concatenate(
        [jnp.concatenate([ref[0, wave], ref[1, wave]], axis=1) for ref in refs], axis=0
    )


def rows_kernel(
    weight_ref, up_ref, own_ref, down_ref, base_re_ref, base_im_ref,
    out_ref, left_ref, right_ref, share_ref, total_ref, high_ref, low_ref,
):
    row_tables(base_re_ref, base_im_ref, high_ref, low_ref)
    total_ref[...] = jnp.zeros_like(total_ref)

    def step(wave):
        re_out, im_out = row_pass(
            stacked_rows((up_ref, own_ref, down_ref), wave), (high_ref[wave], low_ref[wave])
        )
        out_ref[0, wave] = re_out
        out_ref[1, wave] = im_out
        left, right = edges(re_out, im_out)
        left_ref[wave] = left
        right_ref[wave] = right
        total_ref[...] += weight_ref[wave] * (re_out * re_out + im_out * im_out)

    over_waves(step)
    block = total_ref[...] * (1.0 / WAVES)
    for target in range(NW):
        piece = quarter(block, target)
        share_ref[target * NROW : (target + 1) * NROW] = jnp.broadcast_to(
            piece[None], (NROW, 16, 128)
        )


def row_dft_kernel(image_ref, measured_ref, table_ref, out_ref):
    summed = image_ref[0:NROW] + image_ref[NROW : 2 * NROW]
    summed = summed + image_ref[2 * NROW : 3 * NROW]
    summed = (summed + image_ref[3 * NROW : 4 * NROW]).reshape(128, 128)
    known = measured_ref[:, 0:16].reshape(128, 128)
    lane = lane_ids(128) // 32
    top = []
    low = []
    for group in range(4):
        first = pltpu.roll(summed, (128 - 32 * group) % 128, 1)
        third = pltpu.roll(known, (192 - 32 * group) % 128, 1)
        both = jnp.where(lane == 0, first, jnp.where(lane == 2, third, 0.0))
        top.append(both)
        low.append(pltpu.roll(both, 32, 1))
    operand = split(jnp.concatenate(top + low, axis=0))
    out_ref[...] = mm3((table_ref[0], table_ref[1]), operand).reshape(out_ref.shape)


def eight_point(terms, sign):
    if len(terms) == 1:
        return terms
    count = len(terms)
    even = eight_point(terms[0::2], sign)
    odd = eight_point(terms[1::2], sign)
    first, second = [], []
    for n in range(count // 2):
        re_part, im_part = odd[n]
        im_part = im_part if sign > 0 else -im_part
        turn = 8 * n // count
        if turn == 1:
            re_part, im_part = (re_part - im_part) * ROOT, (re_part + im_part) * ROOT
        elif turn == 2:
            re_part, im_part = -im_part, re_part
        elif turn == 3:
            re_part, im_part = -(re_part + im_part) * ROOT, (re_part - im_part) * ROOT
        im_part = im_part if sign > 0 else -im_part
        first.append((even[n][0] + re_part, even[n][1] + im_part))
        second.append((even[n][0] - re_part, even[n][1] - im_part))
    return first + second


def filter_kernel(rows_ref, spec_ref, table_ref, out_ref):
    lane = lane_ids(16) // 32
    blocks = []
    for col in range(NCOL):
        channels = []
        for channel in range(4):
            piece = jnp.zeros((16, 128), F32)
            for wave in range(NW):
                moved = pltpu.roll(rows_ref[col * NW + wave], (32 * (wave - channel)) % 128, 1)
                piece = jnp.where(lane == wave, moved, piece)
            channels.append(piece)
        blocks.append(
            (
                jnp.concatenate([channels[0], channels[2]], axis=0),
                jnp.concatenate([channels[1], channels[3]], axis=0),
            )
        )
    sums = eight_point(blocks, -1)
    scale = 1.0 / (NR * NC)
    back = []
    for n in range(8):
        operand = split(jnp.concatenate(sums[n], axis=0))
        mix = mm3(operand, (table_ref[0, n], table_ref[1, n]))
        freq_re = mix[:32, :128] + mix[32:, 128:]
        freq_im = mix[32:, :128] - mix[:32, 128:]
        image_re, known_re = freq_re[:16], freq_re[16:]
        image_im, known_im = freq_im[:16], freq_im[16:]
        spec_re, spec_im = spec_ref[n, 0:16], spec_ref[n, 16:32]
        blur_re = image_re * spec_re - image_im * spec_im
        blur_im = image_re * spec_im + image_im * spec_re
        rest_re = blur_re - known_re
        rest_im = blur_im - known_im
        pull_re = rest_re * spec_re + rest_im * spec_im
        pull_im = rest_im * spec_re - rest_re * spec_im
        both = jnp.concatenate([blur_re - pull_im, blur_im + pull_re], axis=0) * scale
        mix = mm3(split(both), (table_ref[2, n], table_ref[3, n]))
        back.append((mix[:16, :128] - mix[16:, 128:], mix[:16, 128:] + mix[16:, :128]))
    columns = eight_point(back, 1)
    for col in range(NCOL):
        left, right = edges(*columns[col])
        out_ref[col * NW + 1] = left
        out_ref[(col + 7) % 8 * NW + 3] = left
        out_ref[(col + 1) % 8 * NW] = right
        out_ref[col * NW + 2] = right


def halo_kernel(left_ref, right_ref, out_ref):
    for wave in range(LW):
        out_ref[0, wave], out_ref[1, wave] = halo_parts(left_ref[wave], right_ref[wave])


def row_inverse_kernel(rows_ref, table_ref, out_ref):
    operand = split(rows_ref[...].reshape(NR, 128))
    mix = mm3((table_ref[0], table_ref[1]), operand)
    cos_part, sin_part = mix[:64], mix[64:]
    pulled = sin_part + swapped(cos_part)
    blurred = cos_part - swapped(sin_part)
    both = jnp.where(lane_ids(64) < 64, pulled, swapped(blurred))
    out_ref[...] = jnp.broadcast_to(both[None], out_ref.shape)


def back_columns_kernel(
    images_ref, measured_ref, field_ref, halo_ref, base_re_ref, base_im_ref,
    out_ref, residual_ref, centre_ref, border_ref, high_ref, low_ref,
):
    column_tables(base_re_ref, base_im_ref, high_ref, low_ref)
    low = lane_ids(64) < 64
    first, second = images_ref[1], images_ref[2]
    centre_ref[...] = jnp.where(low, first, swapped(second))
    residual_ref[...] = jnp.where(low, swapped(first), second) - measured_ref[...]
    border_ref[...] = jnp.where(low, images_ref[0], swapped(images_ref[3]))

    def step(wave):
        centre, border = centre_ref[...], border_ref[...]
        out_ref[0, wave], out_ref[1, wave] = column_pass(
            (field_ref[0, wave] * centre, halo_ref[0, wave] * border),
            (-field_ref[1, wave] * centre, -halo_ref[1, wave] * border),
            (high_ref[wave], low_ref[wave]),
        )

    over_waves(step)


def back_rows_kernel(
    weight_ref, up_ref, own_ref, down_ref, base_re_ref, base_im_ref, out_ref, high_ref, low_ref
):
    row_tables(base_re_ref, base_im_ref, high_ref, low_ref)

    def step(wave):
        re_out, im_out = row_pass(
            stacked_rows((up_ref, own_ref, down_ref), wave), (high_ref[wave], low_ref[wave])
        )
        factor = 2.0 * weight_ref[wave]
        out_ref[0, wave] = factor * re_out
        out_ref[1, wave] = -factor * im_out

    over_waves(step)


def params():
    return pltpu.CompilerParams(vmem_limit_bytes=VMEM_LIMIT)


def near(*dims, dtype=F32):
    return pltpu.VMEM(dims, dtype)


def far(*dims, dtype=F32):
    return pltpu.HBM(dims, dtype)


SMEM = pl.BlockSpec(memory_space=pltpu.SMEM)
ANY = pl.BlockSpec(memory_space=pl.ANY)
VM = pl.BlockSpec()


def kept(value):
    return pltpu.with_memory_space_constraint(value, pltpu.HBM)


def loaded(place, table):
    return pl.pallas_call(
        load_kernel,
        in_specs=[SMEM, ANY],
        out_shape=near(*table.shape[1:], dtype=BF16),
        scratch_shapes=[pltpu.SemaphoreType.DMA((1,))],
        compiler_params=params(),
    )(place, kept(jnp.asarray(table)))


def neighbours(value, axis, count, step):
    return lax.ppermute(
        value, axis, [(i, i + step) for i in range(count) if 0 <= i + step < count]
    )


def taps_of(wavelength):
    lane = jnp.arange(256)
    offset = jnp.where(lane < 128, lane, lane - 256).astype(F32)
    spread = jnp.arange(-HALO, HALO + 1).astype(F32)
    norm = 1.0 / jnp.sqrt(jnp.sum(jnp.exp(-2.0 * (spread / HALO) ** 2)))
    amplitude = jnp.where(jnp.abs(offset) <= HALO, jnp.exp(-((offset / HALO) ** 2)) * norm, 0.0)
    phase = offset * offset / (2.0 * wavelength[:, None] * HALO)
    return (amplitude * jnp.cos(phase))[:, None, :], (amplitude * jnp.sin(phase))[:, None, :]


def shards(wavefield, wavelength, weight, spectrum, measured):
    wave_place = lax.axis_index("wave")[None]
    row_place = lax.axis_index("row")[None]
    call = functools.partial(pl.pallas_call, compiler_params=params())
    field, edge, slots = (2, LW, 64, 128), (LW, 64, 128), (NCOL * NW, 16, 128)

    field_held, left_edge, right_edge = call(
        pack_kernel,
        in_specs=[ANY],
        out_shape=(near(*field), far(*edge), far(*edge)),
        scratch_shapes=[pltpu.SemaphoreType.DMA((LW,))],
    )(kept(wavefield))
    from_left = neighbours(right_edge, "col", NCOL, 1)
    from_right = neighbours(left_edge, "col", NCOL, -1)

    base = taps_of(wavelength)
    known_share, mirror, first = call(
        mirror_kernel,
        in_specs=[SMEM, ANY, ANY, ANY],
        out_shape=(near(48, 128), far(2, KB, 128), far(2, 8, 128)),
        scratch_shapes=[
            pltpu.VMEM((64, 128), F32), pltpu.VMEM((2, 64, 128), F32), pltpu.SemaphoreType.DMA((2,)),
        ],
    )(wave_place, kept(measured), kept(spectrum), kept(left_edge))
    mirror = lax.ppermute(mirror, "col", [(i, 7 - i) for i in range(NCOL)])
    first = lax.ppermute(first, "col", [(i, (8 - i) % 8) for i in range(NCOL)])
    known_share = call(share_kernel, in_specs=[SMEM, VM, VM, VM], out_shape=far(NROW, 80, 128))(
        wave_place, known_share, mirror, first
    )
    known = known_share
    known = lax.all_to_all(known, "row", split_axis=0, concat_axis=0, tiled=True)
    spec = call(order_kernel, out_shape=near(8, 32, 128))(
        known, jnp.asarray(column_order()), jnp.asarray(np.eye(128)[::-1].astype(ml_dtypes.bfloat16))
    )

    col_scratch = [pltpu.VMEM((LW, 256, 256), BF16)] * 2
    row_scratch = [pltpu.VMEM((LW, 128, 192), BF16)] * 2
    middle = call(
        columns_kernel,
        in_specs=[VM] * 5 + [ANY],
        out_shape=near(*field),
        scratch_shapes=col_scratch,
    )(field_held, from_left, from_right, *base, kept(known_share))
    from_up = neighbours(middle, "row", NROW, 1)
    from_down = neighbours(middle, "row", NROW, -1)
    propagated, left_edge, right_edge, shares = call(
        rows_kernel,
        in_specs=[SMEM] + [VM] * 5,
        out_shape=(near(*field), far(*edge), far(*edge), far(*slots)),
        scratch_shapes=[pltpu.VMEM((64, 128), F32)] + row_scratch,
    )(weight, from_up, middle, from_down, *base)

    prop_left = neighbours(right_edge, "col", NCOL, 1)
    prop_right = neighbours(left_edge, "col", NCOL, -1)
    prop_halo = call(
        halo_kernel,
        out_shape=near(*field),
        cost_estimate=MEDIUM,
    )(prop_left, prop_right)

    image = lax.all_to_all(shares, ("wave", "row"), split_axis=0, concat_axis=0, tiled=True)
    first_place = jnp.zeros((1,), jnp.int32)
    row_dft = loaded(first_place, np.stack(row_dft_table())[None])
    freq_rows = call(row_dft_kernel, out_shape=far(*slots))(image, known, row_dft)
    freq_rows = lax.all_to_all(freq_rows, ("col", "wave"), split_axis=0, concat_axis=0, tiled=True)

    col_dft = loaded(first_place, np.stack(col_dft_table() + col_inverse_table())[None])
    columns = call(filter_kernel, out_shape=far(*slots))(freq_rows, spec, col_dft)
    columns = lax.all_to_all(columns, ("col", "wave"), split_axis=0, concat_axis=0, tiled=True)

    row_back = loaded(row_place, np.stack(row_inverse_table(), axis=1))
    images = call(row_inverse_kernel, out_shape=far(NW, 64, 128))(columns, row_back)
    images = lax.all_to_all(images, "wave", split_axis=0, concat_axis=0, tiled=True)

    middle, residual = call(
        back_columns_kernel,
        out_shape=(near(*field), far(64, 128)),
        scratch_shapes=[pltpu.VMEM((64, 128), F32)] * 2 + col_scratch,
    )(images, measured, propagated, prop_halo, *base)
    from_up = neighbours(middle, "row", NROW, 1)
    from_down = neighbours(middle, "row", NROW, -1)
    field_grad = call(
        back_rows_kernel,
        in_specs=[SMEM] + [VM] * 5,
        out_shape=far(*field),
        scratch_shapes=row_scratch,
    )(weight, from_up, middle, from_down, *base)
    return field_grad, residual


def solution(mesh):
    placed = (
        P(None, "wave", "row", "col"),
        P("wave"),
        P("wave"),
        P(None, "col", "row"),
        P("row", "col"),
    )
    return jax.shard_map(
        shards,
        mesh=mesh,
        in_specs=placed,
        out_specs=(P(None, "wave", "row", "col"), P("row", "col")),
        check_vma=False,
    )
```

```python
import functools

import jax
import jax.numpy as jnp
import ml_dtypes
import numpy as np
from jax import lax
from jax.experimental import pallas as pl
from jax.experimental.pallas import tpu as pltpu
from jax.sharding import PartitionSpec as P

WAVES = 32
HALO = 64
TR = 64
TC = 128
NR = 512
NC = 1024
NW = 4
NROW = 8
NCOL = 8
LW = WAVES // NW
QC = TC // NW
KB = NR // (NCOL * NW)
STEP = 8
MEDIUM = pl.CostEstimate(flops=1 << 36, bytes_accessed=0, transcendentals=0)
ROOT = float(np.sqrt(0.5))
F32 = jnp.float32
BF16 = jnp.bfloat16
VMEM_LIMIT = 20 * 1024 * 1024


def halves_of(table):
    high = table.astype(ml_dtypes.bfloat16)
    low = (table - high.astype(np.float64)).astype(ml_dtypes.bfloat16)
    return high, low


@functools.lru_cache(None)
def row_dft_table():
    group, block, inner = np.meshgrid(np.arange(4), np.arange(NROW), np.arange(16), indexing="ij")
    rows = (TR * block + 16 * group + inner).reshape(-1)
    angle = 2 * np.pi * (np.arange(NR)[:, None] * rows[None, :] % NR) / NR
    return halves_of(np.concatenate([np.cos(angle), -np.sin(angle)], axis=1))


@functools.lru_cache(None)
def col_dft_table():
    freq = (8 * np.arange(128)[None, :] + np.arange(8)[:, None])[:, None, :]
    angle = 2 * np.pi * (np.arange(128)[None, :, None] * freq % NC) / NC
    return halves_of(np.concatenate([np.cos(angle), np.sin(angle)], axis=2))


@functools.lru_cache(None)
def col_inverse_table():
    freq = (8 * np.arange(128)[None, :] + np.arange(8)[:, None])[:, :, None]
    angle = 2 * np.pi * (np.arange(128)[None, None, :] * freq % NC) / NC
    return halves_of(np.concatenate([np.cos(angle), np.sin(angle)], axis=2))


@functools.lru_cache(None)
def column_order():
    table = np.zeros((128, 128))
    for m in range(16):
        for n in range(8):
            table[8 * m + n, 16 * n + m] = 1.0
    return table.astype(ml_dtypes.bfloat16)


@functools.lru_cache(None)
def row_inverse_table():
    rows = TR * np.arange(NROW)[:, None] + np.arange(TR)[None, :]
    angle = 2 * np.pi * (rows[:, :, None] * np.arange(NR)[None, None, :] % NR) / NR
    return halves_of(np.concatenate([np.cos(angle), np.sin(angle)], axis=1))


def split(values):
    high = values.astype(BF16)
    return high, (values - high.astype(F32)).astype(BF16)


def mm(left, right):
    return jnp.dot(left, right, preferred_element_type=F32)


def mm3(left, right):
    rows = left[0].shape[0]
    most = mm(jnp.concatenate(left, axis=0), right[0])
    return most[:rows] + (most[rows:] + mm(left[0], right[1]))


def three(values):
    high = values.astype(BF16)
    middle, low = split(values - high.astype(F32))
    return high, middle, low


def lane_ids(rows, lanes=128):
    return lax.broadcasted_iota(jnp.int32, (rows, lanes), 1)


def swapped(values):
    return pltpu.roll(values, 64, 1)


def column_taps(base):
    wide = jnp.broadcast_to(base, (128, 256))
    own = pltpu.roll(wide, 0, 1, stride=1, stride_axis=0)[:, :128]
    left = pltpu.roll(wide[:64], 256 - 64, 1, stride=1, stride_axis=0)[:, :128]
    right = pltpu.roll(wide[:64], 128, 1, stride=1, stride_axis=0)[:, :128]
    return jnp.concatenate([own, left, right], axis=0)


def row_taps(base):
    wide = jnp.broadcast_to(base, (64, 256))
    return pltpu.roll(wide, 64, 1, stride=1, stride_axis=0)[:, :192]


def column_pass(parts_re, parts_im, table):
    rows = parts_re[0].shape[0]
    field = jnp.concatenate(
        [jnp.concatenate(parts_re, axis=1), jnp.concatenate(parts_im, axis=1)], axis=0
    )
    mix = mm3(split(field), table)
    return (
        mix[:rows, :128] - mix[rows:, 128:],
        mix[:rows, 128:] + mix[rows:, :128],
    )


def row_pass(stacked, table):
    mix = mm3(table, split(stacked))
    return mix[:64, :128] - mix[64:, 128:], mix[:64, 128:] + mix[64:, :128]


def over_waves(step):
    def body(start, carry):
        for wave in range(STEP):
            step(start * STEP + wave)
        return carry

    lax.fori_loop(0, LW // STEP, body, 0)


def edges(re_part, im_part):
    lane = lane_ids(re_part.shape[0])
    return (
        jnp.where(lane < 64, re_part, swapped(im_part)),
        jnp.where(lane < 64, swapped(re_part), im_part),
    )


def halo_parts(from_left, from_right):
    lane = lane_ids(from_left.shape[0])
    return (
        jnp.where(lane < 64, from_left, swapped(from_right)),
        jnp.where(lane < 64, swapped(from_left), from_right),
    )


def quarter(block, which):
    lane = lane_ids(16)
    out = jnp.zeros((16, 128), F32)
    for group in range(4):
        amount = lax.rem(32 * group - 32 * which + 128, 128)
        moved = pltpu.roll(block[16 * group : 16 * group + 16], amount, 1)
        out = jnp.where(lane // 32 == group, moved, out)
    return out


def fetch(pairs, sems):
    copies = [
        pltpu.make_async_copy(source, target, sems.at[i])
        for i, (source, target) in enumerate(pairs)
    ]
    for copy in copies:
        copy.start()
    return copies


def load_kernel(place_ref, table_ref, out_ref, sems):
    for copy in fetch([(table_ref.at[place_ref[0]], out_ref)], sems):
        copy.wait()


def pack_kernel(field_ref, held_ref, left_ref, right_ref, sems):
    copies = fetch([(field_ref.at[:, wave], held_ref.at[:, wave]) for wave in range(LW)], sems)
    for wave in range(LW):
        copies[wave].wait()
        left, right = edges(held_ref[0, wave], held_ref[1, wave])
        left_ref[wave] = left
        right_ref[wave] = right


def mirror_kernel(
    place_ref, measured_ref, spec_ref, after_ref, share_ref, mirror_ref, first_ref,
    measured_in, spec_in, sems,
):
    copies = fetch([(spec_ref, spec_in), (measured_ref, measured_in)], sems)
    place = place_ref[0]
    row = lax.broadcasted_iota(jnp.int32, (16, 64), 0)
    pick = (lane_ids(16, 64) == 64 - KB * place - row).astype(BF16)
    copies[0].wait()
    start = pl.multiple_of(place * KB, KB)
    for part in range(2):
        mirror_ref[part] = sum(mm(pick, piece) for piece in three(spec_in[part]))
        first_ref[part] = spec_in[part, 0:8]
        share_ref[16 + 16 * part : 32 + 16 * part] = spec_in[part, pl.ds(start, KB)]
    copies[1].wait()
    share_ref[0:16] = quarter(measured_in[...], place)


def share_kernel(place_ref, share_ref, mirror_ref, first_ref, out_ref):
    place = place_ref[0]
    top = lax.broadcasted_iota(jnp.int32, (16, 128), 0) == 0
    rows = [share_ref[...]]
    for part in range(2):
        other = jnp.broadcast_to(first_ref[part, 0:1], (16, 128))
        rows.append(jnp.where(jnp.logical_and(top, place == 0), other, mirror_ref[part]))
    out_ref[...] = jnp.broadcast_to(jnp.concatenate(rows, axis=0)[None], out_ref.shape)


def order_kernel(rows_ref, order_ref, reverse_ref, out_ref):
    order, reverse = order_ref[...], reverse_ref[...]
    lane = lane_ids(64) // 16
    parts = []
    for row in range(NROW):
        parts.append(sum(mm(piece, order) for piece in three(rows_ref[row, 16:80])))
    ordered = []
    for n in range(8):
        out = jnp.zeros((64, 128), F32)
        for row in range(NROW):
            moved = pltpu.roll(parts[row], (16 * (row - n)) % 128, 1)
            out = jnp.where(lane == row, moved, out)
        ordered.append(out)
    for n in range(8):
        back = sum(mm(piece, reverse) for piece in three(ordered[(8 - n) % 8][32:]))
        if n == 0:
            back = pltpu.roll(back, 1, 1)
        out_ref[n, 0:16] = 0.5 * (ordered[n][0:16] + back[0:16])
        out_ref[n, 16:32] = 0.5 * (ordered[n][16:32] - back[16:32])


def column_tables(base_re_ref, base_im_ref, high_ref, low_ref):
    for wave in range(LW):
        high_ref[wave], low_ref[wave] = split(
            jnp.concatenate(
                [column_taps(base_re_ref[wave]), column_taps(base_im_ref[wave])], axis=1
            )
        )


def row_tables(base_re_ref, base_im_ref, high_ref, low_ref):
    for wave in range(LW):
        high_ref[wave], low_ref[wave] = split(
            jnp.concatenate([row_taps(base_re_ref[wave]), row_taps(base_im_ref[wave])], axis=0)
        )


def columns_kernel(
    field_ref, left_ref, right_ref, base_re_ref, base_im_ref, after_ref, out_ref, high_ref, low_ref
):
    column_tables(base_re_ref, base_im_ref, high_ref, low_ref)

    def step(wave):
        halo_re, halo_im = halo_parts(left_ref[wave], right_ref[wave])
        out_ref[0, wave], out_ref[1, wave] = column_pass(
            (field_ref[0, wave], halo_re),
            (field_ref[1, wave], halo_im),
            (high_ref[wave], low_ref[wave]),
        )

    over_waves(step)


def stacked_rows(refs, wave):
    return jnp.concatenate(
        [jnp.concatenate([ref[0, wave], ref[1, wave]], axis=1) for ref in refs], axis=0
    )


def rows_kernel(
    weight_ref, up_ref, own_ref, down_ref, base_re_ref, base_im_ref,
    out_ref, left_ref, right_ref, share_ref, total_ref, high_ref, low_ref,
):
    row_tables(base_re_ref, base_im_ref, high_ref, low_ref)
    total_ref[...] = jnp.zeros_like(total_ref)

    def step(wave):
        re_out, im_out = row_pass(
            stacked_rows((up_ref, own_ref, down_ref), wave), (high_ref[wave], low_ref[wave])
        )
        out_ref[0, wave] = re_out
        out_ref[1, wave] = im_out
        left, right = edges(re_out, im_out)
        left_ref[wave] = left
        right_ref[wave] = right
        total_ref[...] += weight_ref[wave] * (re_out * re_out + im_out * im_out)

    over_waves(step)
    block = total_ref[...] * (1.0 / WAVES)
    for target in range(NW):
        piece = quarter(block, target)
        share_ref[target * NROW : (target + 1) * NROW] = jnp.broadcast_to(
            piece[None], (NROW, 16, 128)
        )


def row_dft_kernel(image_ref, measured_ref, table_ref, out_ref):
    summed = image_ref[0:NROW] + image_ref[NROW : 2 * NROW]
    summed = summed + image_ref[2 * NROW : 3 * NROW]
    summed = (summed + image_ref[3 * NROW : 4 * NROW]).reshape(128, 128)
    known = measured_ref[:, 0:16].reshape(128, 128)
    lane = lane_ids(128) // 32
    top = []
    low = []
    for group in range(4):
        first = pltpu.roll(summed, (128 - 32 * group) % 128, 1)
        third = pltpu.roll(known, (192 - 32 * group) % 128, 1)
        both = jnp.where(lane == 0, first, jnp.where(lane == 2, third, 0.0))
        top.append(both)
        low.append(pltpu.roll(both, 32, 1))
    operand = split(jnp.concatenate(top + low, axis=0))
    out_ref[...] = mm3((table_ref[0], table_ref[1]), operand).reshape(out_ref.shape)


def eight_point(terms, sign):
    if len(terms) == 1:
        return terms
    count = len(terms)
    even = eight_point(terms[0::2], sign)
    odd = eight_point(terms[1::2], sign)
    first, second = [], []
    for n in range(count // 2):
        re_part, im_part = odd[n]
        im_part = im_part if sign > 0 else -im_part
        turn = 8 * n // count
        if turn == 1:
            re_part, im_part = (re_part - im_part) * ROOT, (re_part + im_part) * ROOT
        elif turn == 2:
            re_part, im_part = -im_part, re_part
        elif turn == 3:
            re_part, im_part = -(re_part + im_part) * ROOT, (re_part - im_part) * ROOT
        im_part = im_part if sign > 0 else -im_part
        first.append((even[n][0] + re_part, even[n][1] + im_part))
        second.append((even[n][0] - re_part, even[n][1] - im_part))
    return first + second


def filter_kernel(rows_ref, spec_ref, table_ref, out_ref):
    lane = lane_ids(16) // 32
    blocks = []
    for col in range(NCOL):
        channels = []
        for channel in range(4):
            piece = jnp.zeros((16, 128), F32)
            for wave in range(NW):
                moved = pltpu.roll(rows_ref[col * NW + wave], (32 * (wave - channel)) % 128, 1)
                piece = jnp.where(lane == wave, moved, piece)
            channels.append(piece)
        blocks.append(
            (
                jnp.concatenate([channels[0], channels[2]], axis=0),
                jnp.concatenate([channels[1], channels[3]], axis=0),
            )
        )
    sums = eight_point(blocks, -1)
    scale = 1.0 / (NR * NC)
    back = []
    for n in range(8):
        operand = split(jnp.concatenate(sums[n], axis=0))
        mix = mm3(operand, (table_ref[0, n], table_ref[1, n]))
        freq_re = mix[:32, :128] + mix[32:, 128:]
        freq_im = mix[32:, :128] - mix[:32, 128:]
        image_re, known_re = freq_re[:16], freq_re[16:]
        image_im, known_im = freq_im[:16], freq_im[16:]
        spec_re, spec_im = spec_ref[n, 0:16], spec_ref[n, 16:32]
        blur_re = image_re * spec_re - image_im * spec_im
        blur_im = image_re * spec_im + image_im * spec_re
        rest_re = blur_re - known_re
        rest_im = blur_im - known_im
        pull_re = rest_re * spec_re + rest_im * spec_im
        pull_im = rest_im * spec_re - rest_re * spec_im
        both = jnp.concatenate([blur_re - pull_im, blur_im + pull_re], axis=0) * scale
        mix = mm3(split(both), (table_ref[2, n], table_ref[3, n]))
        back.append((mix[:16, :128] - mix[16:, 128:], mix[:16, 128:] + mix[16:, :128]))
    columns = eight_point(back, 1)
    for col in range(NCOL):
        left, right = edges(*columns[col])
        out_ref[col * NW + 1] = left
        out_ref[(col + 7) % 8 * NW + 3] = left
        out_ref[(col + 1) % 8 * NW] = right
        out_ref[col * NW + 2] = right


def halo_kernel(left_ref, right_ref, out_ref):
    for wave in range(LW):
        out_ref[0, wave], out_ref[1, wave] = halo_parts(left_ref[wave], right_ref[wave])


def row_inverse_kernel(rows_ref, table_ref, out_ref):
    operand = split(rows_ref[...].reshape(NR, 128))
    mix = mm3((table_ref[0], table_ref[1]), operand)
    cos_part, sin_part = mix[:64], mix[64:]
    pulled = sin_part + swapped(cos_part)
    blurred = cos_part - swapped(sin_part)
    both = jnp.where(lane_ids(64) < 64, pulled, swapped(blurred))
    out_ref[...] = jnp.broadcast_to(both[None], out_ref.shape)


def back_columns_kernel(
    images_ref, measured_ref, field_ref, halo_ref, base_re_ref, base_im_ref,
    out_ref, residual_ref, centre_ref, border_ref, high_ref, low_ref,
):
    column_tables(base_re_ref, base_im_ref, high_ref, low_ref)
    low = lane_ids(64) < 64
    first, second = images_ref[1], images_ref[2]
    centre_ref[...] = jnp.where(low, first, swapped(second))
    residual_ref[...] = jnp.where(low, swapped(first), second) - measured_ref[...]
    border_ref[...] = jnp.where(low, images_ref[0], swapped(images_ref[3]))

    def step(wave):
        centre, border = centre_ref[...], border_ref[...]
        out_ref[0, wave], out_ref[1, wave] = column_pass(
            (field_ref[0, wave] * centre, halo_ref[0, wave] * border),
            (-field_ref[1, wave] * centre, -halo_ref[1, wave] * border),
            (high_ref[wave], low_ref[wave]),
        )

    over_waves(step)


def back_rows_kernel(
    weight_ref, up_ref, own_ref, down_ref, base_re_ref, base_im_ref, out_ref, high_ref, low_ref
):
    row_tables(base_re_ref, base_im_ref, high_ref, low_ref)

    def step(wave):
        re_out, im_out = row_pass(
            stacked_rows((up_ref, own_ref, down_ref), wave), (high_ref[wave], low_ref[wave])
        )
        factor = 2.0 * weight_ref[wave]
        out_ref[0, wave] = factor * re_out
        out_ref[1, wave] = -factor * im_out

    over_waves(step)


def params():
    return pltpu.CompilerParams(vmem_limit_bytes=VMEM_LIMIT)


def near(*dims, dtype=F32):
    return pltpu.VMEM(dims, dtype)


def far(*dims, dtype=F32):
    return pltpu.HBM(dims, dtype)


SMEM = pl.BlockSpec(memory_space=pltpu.SMEM)
ANY = pl.BlockSpec(memory_space=pl.ANY)
VM = pl.BlockSpec()


def kept(value):
    return pltpu.with_memory_space_constraint(value, pltpu.HBM)


def loaded(place, table):
    return pl.pallas_call(
        load_kernel,
        in_specs=[SMEM, ANY],
        out_shape=near(*table.shape[1:], dtype=BF16),
        scratch_shapes=[pltpu.SemaphoreType.DMA((1,))],
        compiler_params=params(),
    )(place, kept(jnp.asarray(table)))


def neighbours(value, axis, count, step):
    return lax.ppermute(
        value, axis, [(i, i + step) for i in range(count) if 0 <= i + step < count]
    )


def taps_of(wavelength):
    lane = jnp.arange(256)
    offset = jnp.where(lane < 128, lane, lane - 256).astype(F32)
    spread = jnp.arange(-HALO, HALO + 1).astype(F32)
    norm = 1.0 / jnp.sqrt(jnp.sum(jnp.exp(-2.0 * (spread / HALO) ** 2)))
    amplitude = jnp.where(jnp.abs(offset) <= HALO, jnp.exp(-((offset / HALO) ** 2)) * norm, 0.0)
    phase = offset * offset / (2.0 * wavelength[:, None] * HALO)
    return (amplitude * jnp.cos(phase))[:, None, :], (amplitude * jnp.sin(phase))[:, None, :]


def shards(wavefield, wavelength, weight, spectrum, measured):
    wave_place = lax.axis_index("wave")[None]
    row_place = lax.axis_index("row")[None]
    call = functools.partial(pl.pallas_call, compiler_params=params())
    field, edge, slots = (2, LW, 64, 128), (LW, 64, 128), (NCOL * NW, 16, 128)

    field_held, left_edge, right_edge = call(
        pack_kernel,
        in_specs=[ANY],
        out_shape=(near(*field), far(*edge), far(*edge)),
        scratch_shapes=[pltpu.SemaphoreType.DMA((LW,))],
    )(kept(wavefield))
    from_left = neighbours(right_edge, "col", NCOL, 1)
    from_right = neighbours(left_edge, "col", NCOL, -1)

    base = taps_of(wavelength)
    known_share, mirror, first = call(
        mirror_kernel,
        in_specs=[SMEM, ANY, ANY, ANY],
        out_shape=(near(48, 128), far(2, KB, 128), far(2, 8, 128)),
        scratch_shapes=[
            pltpu.VMEM((64, 128), F32), pltpu.VMEM((2, 64, 128), F32), pltpu.SemaphoreType.DMA((2,)),
        ],
    )(wave_place, kept(measured), kept(spectrum), kept(left_edge))
    mirror = lax.ppermute(mirror, "col", [(i, 7 - i) for i in range(NCOL)])
    first = lax.ppermute(first, "col", [(i, (8 - i) % 8) for i in range(NCOL)])
    known_share = call(share_kernel, in_specs=[SMEM, VM, VM, VM], out_shape=far(NROW, 80, 128))(
        wave_place, known_share, mirror, first
    )
    known = known_share
    known = lax.all_to_all(known, "row", split_axis=0, concat_axis=0, tiled=True)
    spec = call(order_kernel, out_shape=near(8, 32, 128))(
        known, jnp.asarray(column_order()), jnp.asarray(np.eye(128)[::-1].astype(ml_dtypes.bfloat16))
    )

    col_scratch = [pltpu.VMEM((LW, 256, 256), BF16)] * 2
    row_scratch = [pltpu.VMEM((LW, 128, 192), BF16)] * 2
    middle = call(
        columns_kernel,
        in_specs=[VM] * 5 + [ANY],
        out_shape=near(*field),
        scratch_shapes=col_scratch,
    )(field_held, from_left, from_right, *base, kept(known_share))
    from_up = neighbours(middle, "row", NROW, 1)
    from_down = neighbours(middle, "row", NROW, -1)
    propagated, left_edge, right_edge, shares = call(
        rows_kernel,
        in_specs=[SMEM] + [VM] * 5,
        out_shape=(near(*field), far(*edge), far(*edge), far(*slots)),
        scratch_shapes=[pltpu.VMEM((64, 128), F32)] + row_scratch,
    )(weight, from_up, middle, from_down, *base)

    prop_left = neighbours(right_edge, "col", NCOL, 1)
    prop_right = neighbours(left_edge, "col", NCOL, -1)
    prop_halo = call(
        halo_kernel,
        out_shape=near(*field),
        cost_estimate=MEDIUM,
    )(prop_left, prop_right)

    image = lax.all_to_all(shares, ("wave", "row"), split_axis=0, concat_axis=0, tiled=True)
    first_place = jnp.zeros((1,), jnp.int32)
    row_dft = loaded(first_place, np.stack(row_dft_table())[None])
    freq_rows = call(row_dft_kernel, out_shape=far(*slots))(image, known, row_dft)
    freq_rows = lax.all_to_all(freq_rows, ("col", "wave"), split_axis=0, concat_axis=0, tiled=True)

    col_dft = loaded(first_place, np.stack(col_dft_table() + col_inverse_table())[None])
    columns = call(filter_kernel, out_shape=far(*slots))(freq_rows, spec, col_dft)
    columns = lax.all_to_all(columns, ("col", "wave"), split_axis=0, concat_axis=0, tiled=True)

    row_back = loaded(row_place, np.stack(row_inverse_table(), axis=1))
    images = call(row_inverse_kernel, out_shape=far(NW, 64, 128))(columns, row_back)
    images = lax.all_to_all(images, "wave", split_axis=0, concat_axis=0, tiled=True)

    middle, residual = call(
        back_columns_kernel,
        out_shape=(near(*field), far(64, 128)),
        scratch_shapes=[pltpu.VMEM((64, 128), F32)] * 2 + col_scratch,
    )(images, measured, propagated, prop_halo, *base)
    from_up = neighbours(middle, "row", NROW, 1)
    from_down = neighbours(middle, "row", NROW, -1)
    field_grad = call(
        back_rows_kernel,
        in_specs=[SMEM] + [VM] * 5,
        out_shape=far(*field),
        scratch_shapes=row_scratch,
    )(weight, from_up, middle, from_down, *base)
    return field_grad, residual


def solution(mesh):
    placed = (
        P(None, "wave", "row", "col"),
        P("wave"),
        P("wave"),
        P(None, "col", "row"),
        P("row", "col"),
    )
    return jax.shard_map(
        shards,
        mesh=mesh,
        in_specs=placed,
        out_specs=(P(None, "wave", "row", "col"), P("row", "col")),
        check_vma=False,
    )
```

```python
import functools

import jax
import jax.numpy as jnp
import ml_dtypes
import numpy as np
from jax import lax
from jax.experimental import pallas as pl
from jax.experimental.pallas import tpu as pltpu
from jax.sharding import PartitionSpec as P

WAVES = 32
HALO = 64
TR = 64
TC = 128
NR = 512
NC = 1024
NW = 4
NROW = 8
NCOL = 8
LW = WAVES // NW
QC = TC // NW
KB = NR // (NCOL * NW)
STEP = 8
MEDIUM = pl.CostEstimate(flops=1 << 36, bytes_accessed=0, transcendentals=0)
ROOT = float(np.sqrt(0.5))
F32 = jnp.float32
BF16 = jnp.bfloat16
VMEM_LIMIT = 20 * 1024 * 1024


def halves_of(table):
    high = table.astype(ml_dtypes.bfloat16)
    low = (table - high.astype(np.float64)).astype(ml_dtypes.bfloat16)
    return high, low


@functools.lru_cache(None)
def row_dft_table():
    group, block, inner = np.meshgrid(np.arange(4), np.arange(NROW), np.arange(16), indexing="ij")
    rows = (TR * block + 16 * group + inner).reshape(-1)
    angle = 2 * np.pi * (np.arange(NR)[:, None] * rows[None, :] % NR) / NR
    return halves_of(np.concatenate([np.cos(angle), -np.sin(angle)], axis=1))


@functools.lru_cache(None)
def col_dft_table():
    freq = (8 * np.arange(128)[None, :] + np.arange(8)[:, None])[:, None, :]
    angle = 2 * np.pi * (np.arange(128)[None, :, None] * freq % NC) / NC
    return halves_of(np.concatenate([np.cos(angle), np.sin(angle)], axis=2))


@functools.lru_cache(None)
def col_inverse_table():
    freq = (8 * np.arange(128)[None, :] + np.arange(8)[:, None])[:, :, None]
    angle = 2 * np.pi * (np.arange(128)[None, None, :] * freq % NC) / NC
    return halves_of(np.concatenate([np.cos(angle), np.sin(angle)], axis=2))


@functools.lru_cache(None)
def column_order():
    table = np.zeros((128, 128))
    for m in range(16):
        for n in range(8):
            table[8 * m + n, 16 * n + m] = 1.0
    return table.astype(ml_dtypes.bfloat16)


@functools.lru_cache(None)
def row_inverse_table():
    rows = TR * np.arange(NROW)[:, None] + np.arange(TR)[None, :]
    angle = 2 * np.pi * (rows[:, :, None] * np.arange(NR)[None, None, :] % NR) / NR
    return halves_of(np.concatenate([np.cos(angle), np.sin(angle)], axis=1))


def split(values):
    high = values.astype(BF16)
    return high, (values - high.astype(F32)).astype(BF16)


def mm(left, right):
    return jnp.dot(left, right, preferred_element_type=F32)


def mm3(left, right):
    rows = left[0].shape[0]
    most = mm(jnp.concatenate(left, axis=0), right[0])
    return most[:rows] + (most[rows:] + mm(left[0], right[1]))


def three(values):
    high = values.astype(BF16)
    middle, low = split(values - high.astype(F32))
    return high, middle, low


def lane_ids(rows, lanes=128):
    return lax.broadcasted_iota(jnp.int32, (rows, lanes), 1)


def swapped(values):
    return pltpu.roll(values, 64, 1)


def column_taps(base):
    wide = jnp.broadcast_to(base, (128, 256))
    own = pltpu.roll(wide, 0, 1, stride=1, stride_axis=0)[:, :128]
    left = pltpu.roll(wide[:64], 256 - 64, 1, stride=1, stride_axis=0)[:, :128]
    right = pltpu.roll(wide[:64], 128, 1, stride=1, stride_axis=0)[:, :128]
    return jnp.concatenate([own, left, right], axis=0)


def row_taps(base):
    wide = jnp.broadcast_to(base, (64, 256))
    return pltpu.roll(wide, 64, 1, stride=1, stride_axis=0)[:, :192]


def column_pass(parts_re, parts_im, table):
    rows = parts_re[0].shape[0]
    field = jnp.concatenate(
        [jnp.concatenate(parts_re, axis=1), jnp.concatenate(parts_im, axis=1)], axis=0
    )
    mix = mm3(split(field), table)
    return (
        mix[:rows, :128] - mix[rows:, 128:],
        mix[:rows, 128:] + mix[rows:, :128],
    )


def row_pass(stacked, table):
    mix = mm3(table, split(stacked))
    return mix[:64, :128] - mix[64:, 128:], mix[:64, 128:] + mix[64:, :128]


def over_waves(step):
    def body(start, carry):
        for wave in range(STEP):
            step(start * STEP + wave)
        return carry

    lax.fori_loop(0, LW // STEP, body, 0)


def edges(re_part, im_part):
    lane = lane_ids(re_part.shape[0])
    return (
        jnp.where(lane < 64, re_part, swapped(im_part)),
        jnp.where(lane < 64, swapped(re_part), im_part),
    )


def halo_parts(from_left, from_right):
    lane = lane_ids(from_left.shape[0])
    return (
        jnp.where(lane < 64, from_left, swapped(from_right)),
        jnp.where(lane < 64, swapped(from_left), from_right),
    )


def quarter(block, which):
    lane = lane_ids(16)
    out = jnp.zeros((16, 128), F32)
    for group in range(4):
        amount = lax.rem(32 * group - 32 * which + 128, 128)
        moved = pltpu.roll(block[16 * group : 16 * group + 16], amount, 1)
        out = jnp.where(lane // 32 == group, moved, out)
    return out


def fetch(pairs, sems):
    copies = [
        pltpu.make_async_copy(source, target, sems.at[i])
        for i, (source, target) in enumerate(pairs)
    ]
    for copy in copies:
        copy.start()
    return copies


def load_kernel(place_ref, table_ref, out_ref, sems):
    for copy in fetch([(table_ref.at[place_ref[0]], out_ref)], sems):
        copy.wait()


def pack_kernel(field_ref, held_ref, left_ref, right_ref, sems):
    copies = fetch([(field_ref.at[:, wave], held_ref.at[:, wave]) for wave in range(LW)], sems)
    for wave in range(LW):
        copies[wave].wait()
        left, right = edges(held_ref[0, wave], held_ref[1, wave])
        left_ref[wave] = left
        right_ref[wave] = right


def mirror_kernel(
    place_ref, measured_ref, spec_ref, after_ref, share_ref, mirror_ref, first_ref,
    measured_in, spec_in, sems,
):
    copies = fetch([(spec_ref, spec_in), (measured_ref, measured_in)], sems)
    place = place_ref[0]
    row = lax.broadcasted_iota(jnp.int32, (16, 64), 0)
    pick = (lane_ids(16, 64) == 64 - KB * place - row).astype(BF16)
    copies[0].wait()
    start = pl.multiple_of(place * KB, KB)
    for part in range(2):
        mirror_ref[part] = sum(mm(pick, piece) for piece in three(spec_in[part]))
        first_ref[part] = spec_in[part, 0:8]
        share_ref[16 + 16 * part : 32 + 16 * part] = spec_in[part, pl.ds(start, KB)]
    copies[1].wait()
    share_ref[0:16] = quarter(measured_in[...], place)


def share_kernel(place_ref, share_ref, mirror_ref, first_ref, out_ref):
    place = place_ref[0]
    top = lax.broadcasted_iota(jnp.int32, (16, 128), 0) == 0
    rows = [share_ref[...]]
    for part in range(2):
        other = jnp.broadcast_to(first_ref[part, 0:1], (16, 128))
        rows.append(jnp.where(jnp.logical_and(top, place == 0), other, mirror_ref[part]))
    out_ref[...] = jnp.broadcast_to(jnp.concatenate(rows, axis=0)[None], out_ref.shape)


def order_kernel(rows_ref, order_ref, reverse_ref, out_ref):
    order, reverse = order_ref[...], reverse_ref[...]
    lane = lane_ids(64) // 16
    parts = []
    for row in range(NROW):
        parts.append(sum(mm(piece, order) for piece in three(rows_ref[row, 16:80])))
    ordered = []
    for n in range(8):
        out = jnp.zeros((64, 128), F32)
        for row in range(NROW):
            moved = pltpu.roll(parts[row], (16 * (row - n)) % 128, 1)
            out = jnp.where(lane == row, moved, out)
        ordered.append(out)
    for n in range(8):
        back = sum(mm(piece, reverse) for piece in three(ordered[(8 - n) % 8][32:]))
        if n == 0:
            back = pltpu.roll(back, 1, 1)
        out_ref[n, 0:16] = 0.5 * (ordered[n][0:16] + back[0:16])
        out_ref[n, 16:32] = 0.5 * (ordered[n][16:32] - back[16:32])


def column_tables(base_re_ref, base_im_ref, high_ref, low_ref):
    for wave in range(LW):
        high_ref[wave], low_ref[wave] = split(
            jnp.concatenate(
                [column_taps(base_re_ref[wave]), column_taps(base_im_ref[wave])], axis=1
            )
        )


def row_tables(base_re_ref, base_im_ref, high_ref, low_ref):
    for wave in range(LW):
        high_ref[wave], low_ref[wave] = split(
            jnp.concatenate([row_taps(base_re_ref[wave]), row_taps(base_im_ref[wave])], axis=0)
        )


def columns_kernel(
    field_ref, left_ref, right_ref, base_re_ref, base_im_ref, after_ref, out_ref, high_ref, low_ref
):
    column_tables(base_re_ref, base_im_ref, high_ref, low_ref)

    def step(wave):
        halo_re, halo_im = halo_parts(left_ref[wave], right_ref[wave])
        out_ref[0, wave], out_ref[1, wave] = column_pass(
            (field_ref[0, wave], halo_re),
            (field_ref[1, wave], halo_im),
            (high_ref[wave], low_ref[wave]),
        )

    over_waves(step)


def stacked_rows(refs, wave):
    return jnp.concatenate(
        [jnp.concatenate([ref[0, wave], ref[1, wave]], axis=1) for ref in refs], axis=0
    )


def rows_kernel(
    weight_ref, up_ref, own_ref, down_ref, base_re_ref, base_im_ref,
    out_ref, left_ref, right_ref, share_ref, total_ref, high_ref, low_ref,
):
    row_tables(base_re_ref, base_im_ref, high_ref, low_ref)
    total_ref[...] = jnp.zeros_like(total_ref)

    def step(wave):
        re_out, im_out = row_pass(
            stacked_rows((up_ref, own_ref, down_ref), wave), (high_ref[wave], low_ref[wave])
        )
        out_ref[0, wave] = re_out
        out_ref[1, wave] = im_out
        left, right = edges(re_out, im_out)
        left_ref[wave] = left
        right_ref[wave] = right
        total_ref[...] += weight_ref[wave] * (re_out * re_out + im_out * im_out)

    over_waves(step)
    block = total_ref[...] * (1.0 / WAVES)
    for target in range(NW):
        piece = quarter(block, target)
        share_ref[target * NROW : (target + 1) * NROW] = jnp.broadcast_to(
            piece[None], (NROW, 16, 128)
        )


def row_dft_kernel(image_ref, measured_ref, table_ref, out_ref):
    summed = image_ref[0:NROW] + image_ref[NROW : 2 * NROW]
    summed = summed + image_ref[2 * NROW : 3 * NROW]
    summed = (summed + image_ref[3 * NROW : 4 * NROW]).reshape(128, 128)
    known = measured_ref[:, 0:16].reshape(128, 128)
    lane = lane_ids(128) // 32
    top = []
    low = []
    for group in range(4):
        first = pltpu.roll(summed, (128 - 32 * group) % 128, 1)
        third = pltpu.roll(known, (192 - 32 * group) % 128, 1)
        both = jnp.where(lane == 0, first, jnp.where(lane == 2, third, 0.0))
        top.append(both)
        low.append(pltpu.roll(both, 32, 1))
    operand = split(jnp.concatenate(top + low, axis=0))
    out_ref[...] = mm3((table_ref[0], table_ref[1]), operand).reshape(out_ref.shape)


def eight_point(terms, sign):
    if len(terms) == 1:
        return terms
    count = len(terms)
    even = eight_point(terms[0::2], sign)
    odd = eight_point(terms[1::2], sign)
    first, second = [], []
    for n in range(count // 2):
        re_part, im_part = odd[n]
        im_part = im_part if sign > 0 else -im_part
        turn = 8 * n // count
        if turn == 1:
            re_part, im_part = (re_part - im_part) * ROOT, (re_part + im_part) * ROOT
        elif turn == 2:
            re_part, im_part = -im_part, re_part
        elif turn == 3:
            re_part, im_part = -(re_part + im_part) * ROOT, (re_part - im_part) * ROOT
        im_part = im_part if sign > 0 else -im_part
        first.append((even[n][0] + re_part, even[n][1] + im_part))
        second.append((even[n][0] - re_part, even[n][1] - im_part))
    return first + second


def filter_kernel(rows_ref, spec_ref, table_ref, out_ref):
    lane = lane_ids(16) // 32
    blocks = []
    for col in range(NCOL):
        channels = []
        for channel in range(4):
            piece = jnp.zeros((16, 128), F32)
            for wave in range(NW):
                moved = pltpu.roll(rows_ref[col * NW + wave], (32 * (wave - channel)) % 128, 1)
                piece = jnp.where(lane == wave, moved, piece)
            channels.append(piece)
        blocks.append(
            (
                jnp.concatenate([channels[0], channels[2]], axis=0),
                jnp.concatenate([channels[1], channels[3]], axis=0),
            )
        )
    sums = eight_point(blocks, -1)
    scale = 1.0 / (NR * NC)
    back = []
    for n in range(8):
        operand = split(jnp.concatenate(sums[n], axis=0))
        mix = mm3(operand, (table_ref[0, n], table_ref[1, n]))
        freq_re = mix[:32, :128] + mix[32:, 128:]
        freq_im = mix[32:, :128] - mix[:32, 128:]
        image_re, known_re = freq_re[:16], freq_re[16:]
        image_im, known_im = freq_im[:16], freq_im[16:]
        spec_re, spec_im = spec_ref[n, 0:16], spec_ref[n, 16:32]
        blur_re = image_re * spec_re - image_im * spec_im
        blur_im = image_re * spec_im + image_im * spec_re
        rest_re = blur_re - known_re
        rest_im = blur_im - known_im
        pull_re = rest_re * spec_re + rest_im * spec_im
        pull_im = rest_im * spec_re - rest_re * spec_im
        both = jnp.concatenate([blur_re - pull_im, blur_im + pull_re], axis=0) * scale
        mix = mm3(split(both), (table_ref[2, n], table_ref[3, n]))
        back.append((mix[:16, :128] - mix[16:, 128:], mix[:16, 128:] + mix[16:, :128]))
    columns = eight_point(back, 1)
    for col in range(NCOL):
        left, right = edges(*columns[col])
        out_ref[col * NW + 1] = left
        out_ref[(col + 7) % 8 * NW + 3] = left
        out_ref[(col + 1) % 8 * NW] = right
        out_ref[col * NW + 2] = right


def halo_kernel(left_ref, right_ref, out_ref):
    for wave in range(LW):
        out_ref[0, wave], out_ref[1, wave] = halo_parts(left_ref[wave], right_ref[wave])


def row_inverse_kernel(rows_ref, table_ref, out_ref):
    operand = split(rows_ref[...].reshape(NR, 128))
    mix = mm3((table_ref[0], table_ref[1]), operand)
    cos_part, sin_part = mix[:64], mix[64:]
    pulled = sin_part + swapped(cos_part)
    blurred = cos_part - swapped(sin_part)
    both = jnp.where(lane_ids(64) < 64, pulled, swapped(blurred))
    out_ref[...] = jnp.broadcast_to(both[None], out_ref.shape)


def back_columns_kernel(
    images_ref, measured_ref, field_ref, halo_ref, base_re_ref, base_im_ref,
    out_ref, residual_ref, centre_ref, border_ref, high_ref, low_ref,
):
    column_tables(base_re_ref, base_im_ref, high_ref, low_ref)
    low = lane_ids(64) < 64
    first, second = images_ref[1], images_ref[2]
    centre_ref[...] = jnp.where(low, first, swapped(second))
    residual_ref[...] = jnp.where(low, swapped(first), second) - measured_ref[...]
    border_ref[...] = jnp.where(low, images_ref[0], swapped(images_ref[3]))

    def step(wave):
        centre, border = centre_ref[...], border_ref[...]
        out_ref[0, wave], out_ref[1, wave] = column_pass(
            (field_ref[0, wave] * centre, halo_ref[0, wave] * border),
            (-field_ref[1, wave] * centre, -halo_ref[1, wave] * border),
            (high_ref[wave], low_ref[wave]),
        )

    over_waves(step)


def back_rows_kernel(
    weight_ref, up_ref, own_ref, down_ref, base_re_ref, base_im_ref, out_ref, high_ref, low_ref
):
    row_tables(base_re_ref, base_im_ref, high_ref, low_ref)

    def step(wave):
        re_out, im_out = row_pass(
            stacked_rows((up_ref, own_ref, down_ref), wave), (high_ref[wave], low_ref[wave])
        )
        factor = 2.0 * weight_ref[wave]
        out_ref[0, wave] = factor * re_out
        out_ref[1, wave] = -factor * im_out

    over_waves(step)


def params():
    return pltpu.CompilerParams(vmem_limit_bytes=VMEM_LIMIT)


def near(*dims, dtype=F32):
    return pltpu.VMEM(dims, dtype)


def far(*dims, dtype=F32):
    return pltpu.HBM(dims, dtype)


SMEM = pl.BlockSpec(memory_space=pltpu.SMEM)
ANY = pl.BlockSpec(memory_space=pl.ANY)
VM = pl.BlockSpec()


def kept(value):
    return pltpu.with_memory_space_constraint(value, pltpu.HBM)


def loaded(place, table):
    return pl.pallas_call(
        load_kernel,
        in_specs=[SMEM, ANY],
        out_shape=near(*table.shape[1:], dtype=BF16),
        scratch_shapes=[pltpu.SemaphoreType.DMA((1,))],
        compiler_params=params(),
    )(place, kept(jnp.asarray(table)))


def neighbours(value, axis, count, step):
    return lax.ppermute(
        value, axis, [(i, i + step) for i in range(count) if 0 <= i + step < count]
    )


def taps_of(wavelength):
    lane = np.arange(256)
    offset = np.where(lane < 128, lane, lane - 256).astype(np.float64)
    spread = np.arange(-HALO, HALO + 1)
    norm = 1.0 / np.sqrt(np.sum(np.exp(-2.0 * (spread / HALO) ** 2)))
    amplitude = np.where(np.abs(offset) <= HALO, np.exp(-((offset / HALO) ** 2)) * norm, 0.0)
    offset, amplitude = jnp.asarray(offset, F32), jnp.asarray(amplitude, F32)
    phase = offset * offset / (2.0 * wavelength[:, None] * HALO)
    return (amplitude * jnp.cos(phase))[:, None, :], (amplitude * jnp.sin(phase))[:, None, :]


def shards(wavefield, wavelength, weight, spectrum, measured):
    wave_place = lax.axis_index("wave")[None]
    row_place = lax.axis_index("row")[None]
    call = functools.partial(pl.pallas_call, compiler_params=params())
    field, edge, slots = (2, LW, 64, 128), (LW, 64, 128), (NCOL * NW, 16, 128)

    field_held, left_edge, right_edge = call(
        pack_kernel,
        in_specs=[ANY],
        out_shape=(near(*field), far(*edge), far(*edge)),
        scratch_shapes=[pltpu.SemaphoreType.DMA((LW,))],
    )(kept(wavefield))
    from_left = neighbours(right_edge, "col", NCOL, 1)
    from_right = neighbours(left_edge, "col", NCOL, -1)

    base = taps_of(wavelength)
    known_share, mirror, first = call(
        mirror_kernel,
        in_specs=[SMEM, ANY, ANY, ANY],
        out_shape=(near(48, 128), far(2, KB, 128), far(2, 8, 128)),
        scratch_shapes=[
            pltpu.VMEM((64, 128), F32), pltpu.VMEM((2, 64, 128), F32), pltpu.SemaphoreType.DMA((2,)),
        ],
    )(wave_place, kept(measured), kept(spectrum), kept(left_edge))
    mirror = lax.ppermute(mirror, "col", [(i, 7 - i) for i in range(NCOL)])
    first = lax.ppermute(first, "col", [(i, (8 - i) % 8) for i in range(NCOL)])
    known_share = call(share_kernel, in_specs=[SMEM, VM, VM, VM], out_shape=far(NROW, 80, 128))(
        wave_place, known_share, mirror, first
    )
    known = known_share
    known = lax.all_to_all(known, "row", split_axis=0, concat_axis=0, tiled=True)
    spec = call(order_kernel, out_shape=near(8, 32, 128))(
        known, jnp.asarray(column_order()), jnp.asarray(np.eye(128)[::-1].astype(ml_dtypes.bfloat16))
    )

    col_scratch = [pltpu.VMEM((LW, 256, 256), BF16)] * 2
    row_scratch = [pltpu.VMEM((LW, 128, 192), BF16)] * 2
    middle = call(
        columns_kernel,
        in_specs=[VM] * 5 + [ANY],
        out_shape=near(*field),
        scratch_shapes=col_scratch,
    )(field_held, from_left, from_right, *base, kept(known_share))
    from_up = neighbours(middle, "row", NROW, 1)
    from_down = neighbours(middle, "row", NROW, -1)
    propagated, left_edge, right_edge, shares = call(
        rows_kernel,
        in_specs=[SMEM] + [VM] * 5,
        out_shape=(near(*field), far(*edge), far(*edge), far(*slots)),
        scratch_shapes=[pltpu.VMEM((64, 128), F32)] + row_scratch,
    )(weight, from_up, middle, from_down, *base)

    prop_left = neighbours(right_edge, "col", NCOL, 1)
    prop_right = neighbours(left_edge, "col", NCOL, -1)
    prop_halo = call(
        halo_kernel,
        out_shape=near(*field),
        cost_estimate=MEDIUM,
    )(prop_left, prop_right)

    image = lax.all_to_all(shares, ("wave", "row"), split_axis=0, concat_axis=0, tiled=True)
    first_place = jnp.zeros((1,), jnp.int32)
    row_dft = loaded(first_place, np.stack(row_dft_table())[None])
    freq_rows = call(row_dft_kernel, out_shape=far(*slots))(image, known, row_dft)
    freq_rows = lax.all_to_all(freq_rows, ("col", "wave"), split_axis=0, concat_axis=0, tiled=True)

    col_dft = loaded(first_place, np.stack(col_dft_table() + col_inverse_table())[None])
    columns = call(filter_kernel, out_shape=far(*slots))(freq_rows, spec, col_dft)
    columns = lax.all_to_all(columns, ("col", "wave"), split_axis=0, concat_axis=0, tiled=True)

    row_back = loaded(row_place, np.stack(row_inverse_table(), axis=1))
    images = call(row_inverse_kernel, out_shape=far(NW, 64, 128))(columns, row_back)
    images = lax.all_to_all(images, "wave", split_axis=0, concat_axis=0, tiled=True)

    middle, residual = call(
        back_columns_kernel,
        out_shape=(near(*field), far(64, 128)),
        scratch_shapes=[pltpu.VMEM((64, 128), F32)] * 2 + col_scratch,
    )(images, measured, propagated, prop_halo, *base)
    from_up = neighbours(middle, "row", NROW, 1)
    from_down = neighbours(middle, "row", NROW, -1)
    field_grad = call(
        back_rows_kernel,
        in_specs=[SMEM] + [VM] * 5,
        out_shape=far(*field),
        scratch_shapes=row_scratch,
    )(weight, from_up, middle, from_down, *base)
    return field_grad, residual


def solution(mesh):
    placed = (
        P(None, "wave", "row", "col"),
        P("wave"),
        P("wave"),
        P(None, "col", "row"),
        P("row", "col"),
    )
    return jax.shard_map(
        shards,
        mesh=mesh,
        in_specs=placed,
        out_specs=(P(None, "wave", "row", "col"), P("row", "col")),
        check_vma=False,
    )
```
